32 devices in a mesh: dp: 8 (over z, y), grp: 4 (over x, core).
Axes of the slice: x: 2, y: 2, z: 4, core: 2. Of those that a mesh axis runs over, the one named last changes fastest.
Arguments:
- features: bfloat16 [4096, 512], P(('dp', 'grp'))
- loss_scale: bfloat16 [4096], P(('dp', 'grp')), may hold values from 8 to 32
- blocks: int32 [4096, 8], P(('dp', 'grp')), may hold values from 0 to 31, all different within a row; in each aligned block of 128 rows (0 to 127, 128 to 255, ...) at most 48 rows name the same one
- label_col: int32 [4096], P(('dp', 'grp')), may hold values from 0 to 1023
- block_slot: int32 [32], replicated, may hold values from 0 to 31, each once
- centers: bfloat16 [32768, 512], P(('dp', 'grp'))
Outputs:
- loss_out: float32 [4096], P(('dp', 'grp'))
- feature_grad: float32 [4096, 512], P(('dp', 'grp'))
- center_grad: bfloat16 [32768, 512], P(('dp', 'grp'))
The draws below stay inside these ranges and needn't reach their ends.
Inputs may be any that keep to these rules, and one draw needn't show every extreme that they name: Each row names 8 different blocks; the first is the sample's own block. Among the rows of one device no block is named by more than 48 rows, and some block is named by exactly 48. A permutation: block b is stored in rows block_slot[b] * 1024 to block_slot[b] * 1024 + 1023 of centers.
All inputs are finite; a program needn't handle non-finite values.
Results may differ from the reference program's by a relative error of at most 0.0054.
Values may be sent and summed in bfloat16 or wider, within the bound.
A program may use at most 64 MiB of HBM per device.

```python
import math
import jax
import jax.numpy as jnp
import numpy as np
from jax import lax

E = 512
BLOCK = 1024
PICKS = 8
TOK_DEV = 128
NB = 32
SAMPLES = 4096
MOST = 48
CAPB = 1536


def draw_features(key, part):
    base = jax.random.normal(jax.random.fold_in(key, 1), (SAMPLES, E), jnp.float32)
    spread = jnp.exp(jax.random.uniform(jax.random.fold_in(key, 2), (SAMPLES, 1), jnp.float32, jnp.log(2.0), jnp.log(16.0)))
    return (base * spread).astype(jnp.bfloat16)


def draw_centers(key, part):
    base = jax.random.normal(jax.random.fold_in(key, 5), (NB * BLOCK, E), jnp.float32)
    return base.astype(jnp.bfloat16)


def touch_ends(values, key, least, largest):
    longest = values.shape.index(max(values.shape))
    spots = []
    for shift in (0, 1):
        where = [jax.random.randint(jax.random.fold_in(key, axis), (), 0, length) for axis, length in enumerate(values.shape)]
        where[longest] = (where[longest] + shift) % values.shape[longest]
        spots.append(tuple(where))
    return values.at[spots[0]].set(least).at[spots[1]].set(largest)


def levels(own_key, dims, split, least, top_value):
    def one(dim, blocks):
        heights = jax.random.uniform(jax.random.fold_in(jax.random.fold_in(own_key, 6), dim), (blocks,), jnp.float32, least / len(split), top_value / len(split))
        return jnp.repeat(jnp.exp(heights), dims[dim] // blocks).reshape((-1,) + (1,) * (len(dims) - dim - 1))

    gain = one(*split[0])
    for cut in split[1:]:
        gain = gain * one(*cut)
    return gain


def routed_block(key, own, number, rows, count, top, most, skew):
    order = jax.random.permutation(key, count)
    packed, common = portions_of(count, rows * top, most, skew, True), portions_of(count, rows * top, most, skew, False)
    places = jnp.arange(count)

    def named(tallies, turn):
        used = int((tallies > 0).sum())
        fixed = max(1, used // 4)
        moved = fixed + (places - fixed + turn * (used - fixed)) % max(1, count - fixed)
        return jnp.zeros((count,), jnp.int32).at[order[jnp.where(places < fixed, places, moved)]].set(jnp.asarray(tallies, jnp.int32))

    tallies = jnp.where(number % 4 == 0, named(packed, number // 4), named(common, number - number // 4 - 1))
    mixed = jax.random.permutation(jax.random.fold_in(own, 3), count)
    donor, receiver = mixed[0:count // 2 * 2:2], mixed[1:count // 2 * 2:2]
    margin = jnp.minimum(tallies[donor] - 1, most - tallies[receiver]) // 2
    margin = jnp.where((donor == order[0]) | (receiver == order[0]) | (tallies[receiver] == 0), 0, jnp.maximum(margin, 0))
    moved = jax.random.randint(jax.random.fold_in(own, 4), (count // 2,), 0, 1 << 20) % (margin + 1)
    tallies = tallies.at[donor].add(-moved).at[receiver].add(moved)
    members = jnp.searchsorted(jnp.cumsum(tallies), jnp.arange(rows * top), side="right").astype(jnp.int32)
    grid = members.reshape(top, rows).T
    grid = grid[jax.random.permutation(jax.random.fold_in(own, 1), rows)]
    turn = jax.random.randint(jax.random.fold_in(own, 2), (rows, 1), 0, top)
    return jnp.take_along_axis(grid, (jnp.arange(top)[None, :] + turn) % top, axis=1)


def portions_of(number_of, total, most, slope, full):
    portions = [(1 << 20) // math.isqrt(grade ** slope) + 1 for grade in range(1, number_of + 1)]
    largest = most if full else min(most, max(-(-total // number_of), total * portions[0] // sum(portions)))
    least = 1 if total - largest >= number_of - 1 else 0
    counts, rest = [largest] + [least] * (number_of - 1), total - largest - least * (number_of - 1)
    while rest > 0:
        movable = [i for i in range(1, number_of) if counts[i] < largest] or [i for i in range(1, number_of) if counts[i] < most]
        pool, budget = sum([portions[i] for i in movable]), rest
        for i in movable:
            more = min(most - counts[i], max(1, budget * portions[i] // pool), rest)
            counts[i] = counts[i] + more
            rest = rest - more
    return np.array(counts)


def setup_inputs(seed: int = 0) -> dict:
    keys = jax.random.split(jax.random.key(seed), 7)
    features = draw_features(jax.random.fold_in(keys[6], 71), 0)
    loss_scale = jnp.clip(jnp.exp(math.log(32.0) - 1.3862944 * jax.random.uniform(keys[1], (SAMPLES,), jnp.float32) ** levels(keys[1], (SAMPLES,), ((0, 32),), -0.2, 0.2)), 8.0, 32.0).astype(jnp.bfloat16)
    blocks_keys = jax.random.split(jax.random.fold_in(keys[2], 1), SAMPLES // TOK_DEV)
    blocks_turns = jax.random.permutation(jax.random.fold_in(keys[2], 3), SAMPLES // TOK_DEV)
    blocks = jax.vmap(lambda own, number: routed_block(jax.random.fold_in(keys[2], 2), own, number, TOK_DEV, NB, PICKS, MOST, 2))(blocks_keys, blocks_turns).reshape((SAMPLES, PICKS))
    label_col = touch_ends(jax.random.randint(keys[3], (SAMPLES,), 0, BLOCK), jax.random.fold_in(keys[3], 1), 0, BLOCK - 1).astype(jnp.int32)
    block_slot = jax.random.permutation(keys[4], NB).astype(jnp.int32)
    centers = draw_centers(jax.random.fold_in(keys[6], 71), 0)
    return {"features": features, "loss_scale": loss_scale, "blocks": blocks, "label_col": label_col, "block_slot": block_slot, "centers": centers}


MARGIN = 0.35
LOGIT_SCALE = 64.0
EPSILON = 1e-06
FLOOR_MAX = -1e+30

def normalize(block_w):
    widened = block_w.astype(jnp.float32)
    lengths = jnp.sqrt(lax.optimization_barrier(jnp.sum(widened * widened, axis=1)) + EPSILON)
    unit_rows = widened / lengths[:, None]
    return (unit_rows.astype(jnp.bfloat16), unit_rows, lengths)

def block_logits(rows_x, normed, columns):
    scores = lax.dot_general(rows_x, normed, (((1,), (1,)), ((), ())), preferred_element_type=jnp.float32)
    positive = lax.broadcasted_iota(jnp.int32, scores.shape, 1) == columns[:, None]
    scores = LOGIT_SCALE * scores - jnp.where(positive, LOGIT_SCALE * MARGIN, 0.0)
    return (scores, positive)

def center_terms(scores, positive, rows_x, normed, unit_rows, lengths, gains, is_valid, row_peak, row_denom):
    probs_row = jnp.exp(scores - row_peak[:, None]) / row_denom[:, None]
    weights = gains.astype(jnp.float32)[:, None] * (probs_row - positive.astype(jnp.float32))
    weights = jnp.where(is_valid[:, None], weights, 0.0).astype(jnp.bfloat16)
    returned = LOGIT_SCALE * jnp.dot(weights, normed, preferred_element_type=jnp.float32)
    unit_grad = LOGIT_SCALE * lax.dot_general(weights, rows_x, (((0,), (0,)), ((), ())), preferred_element_type=jnp.float32)
    along_unit = lax.optimization_barrier(jnp.sum(unit_rows * unit_grad, axis=1, keepdims=True))
    grad_rows = ((unit_grad - unit_rows * along_unit) / lengths[:, None]).astype(jnp.bfloat16)
    return (returned, grad_rows)

def pair_table(blocks, label_col, block_slot):
    pair_count = SAMPLES * PICKS
    pair_iota = jnp.arange(pair_count, dtype=jnp.int32)
    sample_ids = pair_iota // PICKS
    pick_ids = pair_iota % PICKS
    flat_blocks = blocks.reshape(-1).astype(jnp.int32)
    source = sample_ids // TOK_DEV
    within = sample_ids % TOK_DEV
    sort_keys = (source * NB + flat_blocks) * TOK_DEV + within
    ordering = jnp.argsort(sort_keys, stable=True).astype(jnp.int32)
    sorted_groups = sort_keys[ordering] // TOK_DEV
    starts = jnp.concatenate([jnp.ones((1,), bool), sorted_groups[1:] != sorted_groups[:-1]])
    group_start = lax.cummax(jnp.where(starts, pair_iota, 0), axis=0)
    rank_of = jnp.zeros((pair_count,), jnp.int32).at[ordering].set(pair_iota - group_start)
    slot_ids = block_slot[flat_blocks].astype(jnp.int32)
    index = slot_ids * CAPB + source * MOST + rank_of
    ids_table = jnp.full((NB * CAPB,), SAMPLES, jnp.int32).at[index].set(sample_ids)
    col_values = jnp.where(pick_ids == 0, label_col[sample_ids].astype(jnp.int32), -1)
    col_table = jnp.full((NB * CAPB,), -1, jnp.int32).at[index].set(col_values)
    return (ids_table.reshape(NB, CAPB), col_table.reshape(NB, CAPB))

def reference(features, loss_scale, blocks, label_col, block_slot, centers):
    ids_table, col_table = pair_table(blocks, label_col, block_slot)
    normed_feat, unit_feat, feat_norm = normalize(features)
    padded = jnp.concatenate([normed_feat, jnp.zeros((1, E), jnp.bfloat16)])
    scales = jnp.concatenate([loss_scale.astype(jnp.float32), jnp.zeros((1,), jnp.float32)])
    blocks_w = centers.reshape(NB, BLOCK, E)

    def first_pass(slot_idx):
        row_ids = ids_table[slot_idx]
        normed, unit_rows, lengths = normalize(blocks_w[slot_idx])
        scores, positive = block_logits(padded[row_ids], normed, col_table[slot_idx])
        highest = lax.optimization_barrier(jnp.max(scores, axis=1))
        totals = lax.optimization_barrier(jnp.sum(jnp.exp(scores - highest[:, None]), axis=1))
        picked = lax.optimization_barrier(jnp.sum(jnp.where(positive, scores, 0.0), axis=1))
        return (highest, totals, picked)
    highs, totals, picks = lax.map(first_pass, jnp.arange(NB, dtype=jnp.int32))
    flat_ids = ids_table.reshape(-1)
    highs = highs.reshape(-1)
    sample_peak = jnp.full((SAMPLES + 1,), FLOOR_MAX, jnp.float32).at[flat_ids].max(highs)
    sample_denom = jnp.zeros((SAMPLES + 1,), jnp.float32).at[flat_ids].add(totals.reshape(-1) * jnp.exp(highs - sample_peak[flat_ids]))
    target = jnp.zeros((SAMPLES + 1,), jnp.float32).at[flat_ids].add(picks.reshape(-1))
    loss_all = sample_peak + jnp.log(sample_denom) - target

    def second_pass(grad_acc, slot_idx):
        row_ids = ids_table[slot_idx]
        normed, unit_rows, lengths = normalize(blocks_w[slot_idx])
        rows_x = padded[row_ids]
        scores, positive = block_logits(rows_x, normed, col_table[slot_idx])
        returned, grad_rows = center_terms(scores, positive, rows_x, normed, unit_rows, lengths, scales[row_ids], row_ids < SAMPLES, sample_peak[row_ids], sample_denom[row_ids])
        return (grad_acc.at[row_ids].add(returned), grad_rows)
    grad_init = jnp.zeros((SAMPLES + 1, E), jnp.float32)
    grad_acc, center_rows = lax.scan(second_pass, grad_init, jnp.arange(NB, dtype=jnp.int32))
    unit_fgrad = grad_acc[:SAMPLES]
    along = lax.optimization_barrier(jnp.sum(unit_feat * unit_fgrad, axis=1, keepdims=True))
    feature_grad = (unit_fgrad - unit_feat * along) / feat_norm[:, None]
    return (loss_all[:SAMPLES], feature_grad, center_rows.reshape(NB * BLOCK, E))
```

```python
import functools

import jax
import jax.numpy as jnp
from jax import lax
from jax.experimental import pallas as pl
from jax.experimental.pallas import tpu as pltpu
from jax.sharding import PartitionSpec as P

BLOCK = 1024


MARGIN = 0.35
LOGIT_SCALE = 64.0
EPSILON = 1e-06


def normalize(block_w):
    widened = block_w.astype(jnp.float32)
    lengths = jnp.sqrt(jnp.sum(widened * widened, axis=1) + EPSILON)
    unit_rows = widened / lengths[:, None]
    return (unit_rows.astype(jnp.bfloat16), unit_rows, lengths)


def normalize_block(block_w):
    squares = jnp.einsum("re,re->r", block_w, block_w, preferred_element_type=jnp.float32)
    lengths = jnp.sqrt(squares + EPSILON)
    unit_rows = block_w.astype(jnp.float32) / lengths[:, None]
    scaled = unit_rows.astype(jnp.bfloat16) * LOGIT_SCALE
    return (scaled, unit_rows, lengths)


def block_logits(rows_x, scaled_centers, columns):
    width = scaled_centers.shape[0]
    scores = lax.dot_general(
        rows_x, scaled_centers, (((1,), (1,)), ((), ())), preferred_element_type=jnp.float32
    )
    row_iota = jnp.arange(rows_x.shape[0], dtype=jnp.int32)
    target_cols = jnp.where(columns >= 0, columns, width)
    scores = scores.at[row_iota, target_cols].add(-LOGIT_SCALE * MARGIN, mode="drop")
    picked = jnp.where(columns >= 0, scores[row_iota, jnp.maximum(columns, 0)], 0.0)
    return (scores, picked)


def center_terms(exps, factor, columns, gains, rows_x, scaled_centers, unit_rows, lengths):
    width = scaled_centers.shape[0]
    row_iota = jnp.arange(exps.shape[0], dtype=jnp.int32)
    target_cols = jnp.where(columns >= 0, columns, width)
    weights = exps * factor[:, None]
    weights = (
        weights.at[row_iota, target_cols]
        .add(-gains.astype(jnp.float32), mode="drop")
        .astype(jnp.bfloat16)
    )
    returned = jnp.dot(weights, scaled_centers, preferred_element_type=jnp.float32)
    scaled_rows = rows_x * LOGIT_SCALE
    unit_grad = lax.dot_general(
        weights, scaled_rows, (((0,), (0,)), ((), ())), preferred_element_type=jnp.float32
    )
    along_unit = jnp.einsum("re,re->r", unit_rows, unit_grad)
    grad_rows = ((unit_grad - unit_rows * along_unit[:, None]) / lengths[:, None]).astype(
        jnp.bfloat16
    )
    return (returned, grad_rows)


def route_rows(rows_out, gains_out, sample_tags, col_tags):
    return (
        lax.all_to_all(
            lax.all_to_all(rows_out, "dp", split_axis=2, concat_axis=2, tiled=True),
            "grp",
            split_axis=1,
            concat_axis=1,
            tiled=True,
        ),
        lax.all_to_all(
            lax.all_to_all(gains_out, "dp", split_axis=2, concat_axis=2, tiled=True),
            "grp",
            split_axis=1,
            concat_axis=1,
            tiled=True,
        ),
        lax.all_to_all(
            lax.all_to_all(sample_tags, "dp", split_axis=2, concat_axis=2, tiled=True),
            "grp",
            split_axis=1,
            concat_axis=1,
            tiled=True,
        ),
        lax.all_to_all(
            lax.all_to_all(col_tags, "dp", split_axis=2, concat_axis=2, tiled=True),
            "grp",
            split_axis=1,
            concat_axis=1,
            tiled=True,
        ),
    )


def route_grads(returned):
    return lax.all_to_all(
        lax.all_to_all(returned, "dp", split_axis=2, concat_axis=2, tiled=True),
        "grp",
        split_axis=1,
        concat_axis=1,
        tiled=True,
    )


def on_device(features, loss_scale, blocks, label_col, block_slot, centers):
    dp_count = lax.axis_size("dp")
    groups = lax.axis_size("grp")
    sample_count, feature_width = features.shape
    pick_count = blocks.shape[1]
    block_total = block_slot.shape[0]
    per_device = centers.shape[0] // BLOCK
    quota = (sample_count * pick_count + block_total - 1) // block_total
    capacity_most = quota + max(1, quota // 2)
    pair_count = sample_count * pick_count
    layout = (per_device, groups, dp_count, capacity_most)
    slot_total = per_device * groups * dp_count * capacity_most
    capacity = groups * dp_count * capacity_most
    normed_feat, unit_feat, feat_norm = normalize(features)
    flat_blocks = blocks.reshape(-1)
    matches = flat_blocks[:, None] == lax.broadcasted_iota(jnp.int32, (pair_count, block_total), 1)
    slot_ids = jnp.sum(jnp.where(matches, block_slot[None, :], 0), axis=1)
    owner_flat = slot_ids // per_device
    local_block = slot_ids % per_device
    owner_grp = owner_flat % groups
    owner_dp = owner_flat // groups
    sample_of = lax.broadcasted_iota(jnp.int32, (sample_count, pick_count), 0).reshape(-1)
    pick_of = lax.broadcasted_iota(jnp.int32, (sample_count, pick_count), 1).reshape(-1)
    earlier = (flat_blocks[:, None] == flat_blocks[None, :]) & (
        sample_of[None, :] < sample_of[:, None]
    )
    rank_of = jnp.sum(earlier.astype(jnp.int32), axis=1)
    places = ((local_block * groups + owner_grp) * dp_count + owner_dp) * capacity_most + rank_of
    rows_out = (
        jnp.zeros((slot_total, feature_width), jnp.bfloat16)
        .at[places]
        .set(jnp.repeat(normed_feat, pick_count, axis=0))
    )
    gains_out = (
        jnp.zeros((slot_total,), jnp.bfloat16).at[places].set(jnp.repeat(loss_scale, pick_count))
    )
    sample_tags = jnp.full((slot_total,), -1, jnp.int32).at[places].set(sample_of)
    col_values = jnp.where(pick_of == 0, jnp.repeat(label_col, pick_count), -1)
    col_tags = jnp.full((slot_total,), -1, jnp.int32).at[places].set(col_values)
    rows_in, gains_in, samples_in, cols_in = route_rows(
        rows_out.reshape(layout + (feature_width,)),
        gains_out.reshape(layout),
        sample_tags.reshape(layout),
        col_tags.reshape(layout),
    )
    local_idx = 0
    scaled_centers, unit_rows, lengths = normalize_block(centers)
    rows_x = rows_in[local_idx].reshape(capacity, feature_width)
    columns = cols_in[local_idx].reshape(capacity)
    scores, picked = block_logits(rows_x, scaled_centers, columns)
    tag_rows = samples_in[local_idx].reshape(capacity)
    gains = gains_in[local_idx].reshape(capacity)
    local_data = [
        (scores, picked, rows_x, scaled_centers, unit_rows, lengths, gains, tag_rows, columns)
    ]
    entry = local_data[0]
    highest = jnp.max(entry[0], axis=1)
    exps = jnp.exp(entry[0] - highest[:, None])
    exps_list = [exps]
    highs = [highest]
    totals = [jnp.sum(exps, axis=1)]
    picks_list = [entry[1]]
    back_high, back_total, back_pick = (
        lax.all_to_all(
            lax.all_to_all(
                jnp.stack(highs).reshape(layout), "dp", split_axis=2, concat_axis=2, tiled=True
            ),
            "grp",
            split_axis=1,
            concat_axis=1,
            tiled=True,
        ),
        lax.all_to_all(
            lax.all_to_all(
                jnp.stack(totals).reshape(layout), "dp", split_axis=2, concat_axis=2, tiled=True
            ),
            "grp",
            split_axis=1,
            concat_axis=1,
            tiled=True,
        ),
        lax.all_to_all(
            lax.all_to_all(
                jnp.stack(picks_list).reshape(layout), "dp", split_axis=2, concat_axis=2, tiled=True
            ),
            "grp",
            split_axis=1,
            concat_axis=1,
            tiled=True,
        ),
    )
    pair_high = back_high.reshape(-1)[places].reshape(sample_count, pick_count)
    pair_total = back_total.reshape(-1)[places].reshape(sample_count, pick_count)
    pair_pick = back_pick.reshape(-1)[places].reshape(sample_count, pick_count)
    sample_peak = jnp.max(pair_high, axis=1)
    sample_denom = jnp.sum(pair_total * jnp.exp(pair_high - sample_peak[:, None]), axis=1)
    target = jnp.sum(pair_pick, axis=1)
    peak_out = (
        jnp.zeros((slot_total,), jnp.float32).at[places].set(jnp.repeat(sample_peak, pick_count))
    )
    denom_out = (
        jnp.ones((slot_total,), jnp.float32).at[places].set(jnp.repeat(sample_denom, pick_count))
    )
    peak_in, denom_in = (
        lax.all_to_all(
            lax.all_to_all(peak_out.reshape(layout), "dp", split_axis=2, concat_axis=2, tiled=True),
            "grp",
            split_axis=1,
            concat_axis=1,
            tiled=True,
        ),
        lax.all_to_all(
            lax.all_to_all(
                denom_out.reshape(layout), "dp", split_axis=2, concat_axis=2, tiled=True
            ),
            "grp",
            split_axis=1,
            concat_axis=1,
            tiled=True,
        ),
    )
    local_idx = 0
    row_peak = peak_in[local_idx].reshape(capacity)
    row_denom = denom_in[local_idx].reshape(capacity)
    gains = local_data[local_idx][6].astype(jnp.float32)
    factors = [gains * jnp.exp(highs[local_idx] - row_peak) / row_denom]
    loss_out = sample_peak + jnp.log(sample_denom) - target
    local_idx = 0
    entry = local_data[local_idx]
    returned, grad_rows = center_terms(
        exps_list[local_idx],
        factors[local_idx],
        entry[8],
        entry[6],
        entry[2],
        entry[3],
        entry[4],
        entry[5],
    )
    returned_list = [returned]
    back_grads = route_grads(jnp.stack(returned_list).reshape(layout + (feature_width,)))
    pair_grads = back_grads.reshape(slot_total, feature_width)[places].reshape(
        sample_count, pick_count, feature_width
    )
    unit_fgrad = jnp.sum(pair_grads, axis=1)
    along = jnp.sum(unit_feat * unit_fgrad, axis=1, keepdims=True)
    feature_grad = (unit_fgrad - unit_feat * along) / feat_norm[:, None]
    return (loss_out, feature_grad, grad_rows)


MESH = pl.DeviceIdType.MESH
VMEM = pl.BlockSpec(memory_space=pltpu.VMEM)
SMEM = pl.BlockSpec(memory_space=pltpu.SMEM)
TAG_ROWS = 16
SPLIT = 32
VMEM_LIMIT = 56 * 1024 * 1024


class Place:
    def __init__(self, depth):
        dp, grp = lax.axis_index("dp"), lax.axis_index("grp")
        self.depth = depth
        self.z, y = lax.div(dp, 2), lax.rem(dp, 2)
        x, self.c = lax.div(grp, 2), lax.rem(grp, 2)
        self.a = y + self.c * (x - y)
        self.b = x + self.c * (y - x)
        self.me = dp * 4 + grp

    def device(self, z, a, b, c):
        y, x = a + c * (b - a), b + c * (a - b)
        return (z * 2 + y, x * 2 + c)

    def origin(self, z, a, b, c):
        dp, grp = self.device(z, a, b, c)
        return dp * 4 + grp

    def up(self):
        return self.device(self.z + 1, self.a, self.b, self.c)

    def down(self):
        return self.device(self.z - 1, self.a, self.b, self.c)

    def first(self):
        return self.device(self.z, 1 - self.a, self.b, self.c)

    def second(self):
        return self.device(self.z, self.a, 1 - self.b, self.c)

    def sibling(self):
        return self.device(self.z, self.b, self.a, 1 - self.c)

    def inside(self, offset):
        if offset == 0:
            return None
        return self.z + offset < self.depth if offset > 0 else self.z + offset >= 0

    def when(self, offset, body):
        if offset == 0:
            body()
        else:
            pl.when(self.inside(offset))(body)


def offsets_at(distance):
    return [0] if distance == 0 else [-distance, distance]


def greet(place):
    barrier = pltpu.get_barrier_semaphore()
    for target in (place.sibling(), place.first(), place.second()):
        pl.semaphore_signal(barrier, inc=1, device_id=target, device_id_type=MESH)

    @pl.when(place.z > 0)
    def _():
        pl.semaphore_signal(barrier, inc=1, device_id=place.down(), device_id_type=MESH)

    @pl.when(place.z < place.depth - 1)
    def _():
        pl.semaphore_signal(barrier, inc=1, device_id=place.up(), device_id_type=MESH)

    last = place.depth - 1
    below, above = lax.div(place.z + last, place.depth), lax.div(2 * last - place.z, place.depth)
    pl.semaphore_wait(barrier, 3 + below + above)


UP, DOWN, FIRST, SECOND, SIB = range(5)


def gather_kernel(depth, x_ref, tags_ref, g_ref, send, recv):
    place = Place(depth)
    rows = x_ref.shape[0]
    widened = x_ref[...].astype(jnp.float32)
    lengths = jnp.sqrt(jnp.sum(widened * widened, axis=1, keepdims=True) + EPSILON)
    g_ref[place.me, 0:rows, :] = (widened / lengths).astype(jnp.bfloat16)
    g_ref[place.me, rows : rows + TAG_ROWS, :] = tags_ref[...]
    greet(place)

    def copy(slot, way, target):
        return pltpu.make_async_remote_copy(
            src_ref=g_ref.at[slot],
            dst_ref=g_ref.at[slot],
            send_sem=send.at[way, slot],
            recv_sem=recv.at[slot],
            device_id=target,
            device_id_type=MESH,
        )

    def arrived(slot):
        copy(slot, SIB, place.sibling()).wait_recv()

    z, a, b, c = place.z, place.a, place.b, place.c

    def along_z(offset, act):
        slot = place.origin(z + offset, a, b, c)
        if offset <= 0:
            pl.when(z < depth - 1)(lambda: act(copy(slot, UP, place.up())))
        if offset >= 0:
            pl.when(z > 0)(lambda: act(copy(slot, DOWN, place.down())))

    def spread(slot, ways, act):
        if FIRST in ways:
            act(copy(slot, FIRST, place.first()))
        if SECOND in ways:
            act(copy(slot, SECOND, place.second()))
        act(copy(slot, SIB, place.sibling()))

    def events():
        for r in range(depth + 2):
            if r < depth:
                for off in offsets_at(r):
                    yield off, 0
            if 1 <= r <= depth:
                for off in offsets_at(r - 1):
                    yield off, 1
                    yield off, 2
            if 2 <= r <= depth + 1:
                for off in offsets_at(r - 2):
                    yield off, 3

    def handle(off, kind, act, wait):
        def body():
            slot = place.origin(
                z + off, 1 - a if kind & 1 else a, 1 - b if kind & 2 else b, c
            )
            if wait and (off != 0 or kind != 0):
                arrived(slot)
            if kind == 0:
                along_z(off, act)
            spread(slot, ((FIRST, SECOND), (SECOND,), (), ())[kind], act)

        place.when(off, body)

    for off, kind in events():
        handle(off, kind, lambda item: item.start(), True)
    for off, kind in events():

        def other():
            arrived(
                place.origin(
                    z + off, 1 - b if kind & 1 else b, 1 - a if kind & 2 else a, 1 - c
                )
            )

        place.when(off, other)
    for off, kind in events():
        handle(off, kind, lambda item: item.wait_send(), False)


def gather_rows(depth, devices, features, tags):
    rows, width = features.shape
    return pl.pallas_call(
        functools.partial(gather_kernel, depth),
        out_shape=jax.ShapeDtypeStruct((devices, rows + TAG_ROWS, width), jnp.bfloat16),
        in_specs=[VMEM, VMEM],
        out_specs=VMEM,
        scratch_shapes=[
            pltpu.SemaphoreType.DMA((5, devices)),
            pltpu.SemaphoreType.DMA((devices,)),
        ],
        compiler_params=pltpu.CompilerParams(
            collective_id=0, has_side_effects=True, vmem_limit_bytes=VMEM_LIMIT
        ),
        name="gather_rows",
    )(features, tags)


def chosen(rank_ref, o, most):
    rank = rank_ref[pl.ds(o, 1), :]
    shape = (most, rank.shape[1])
    return lax.broadcasted_iota(jnp.int32, shape, 0).astype(jnp.float32) == rank


def center_parts(c_ref):
    widened = c_ref[...].astype(jnp.float32)
    lengths = jnp.sqrt(jnp.sum(widened * widened, axis=1, keepdims=True) + EPSILON)
    return widened / lengths, lengths


def scores_kernel(
    most, block_ref, g_ref, c_ref, xc_ref, e_ref, part_ref, pick_ref, rank_ref, gain_ref, colc_ref, cn_ref, col_ref, sum_ref, tgt_ref
):
    devices, rows = g_ref.shape[0], g_ref.shape[1] - TAG_ROWS
    width = c_ref.shape[0]
    mine = block_ref[0].astype(jnp.float32)
    cn_ref[...] = (center_parts(c_ref)[0].astype(jnp.bfloat16) * LOGIT_SCALE).astype(jnp.bfloat16)
    tags = g_ref[:, rows : rows + TAG_ROWS, 0:rows].astype(jnp.float32)
    place = lax.broadcasted_iota(jnp.int32, tags.shape, 1)
    hit = tags == mine

    def row(n):
        return jnp.sum(jnp.where(place == n, tags, 0.0), axis=1)

    named = jnp.sum(jnp.where(hit & (place < 8), 1.0, 0.0), axis=1)
    own = jnp.sum(jnp.where(hit & (place == 0), 1.0, 0.0), axis=1)
    earlier = lax.broadcasted_iota(jnp.int32, (rows, rows), 0) < lax.broadcasted_iota(jnp.int32, (rows, rows), 1)
    ahead = jnp.dot(
        named.astype(jnp.bfloat16),
        jnp.where(earlier, 1.0, 0.0).astype(jnp.bfloat16),
        preferred_element_type=jnp.float32,
    )
    rank_ref[...] = jnp.where(named > 0.0, ahead, -1.0)
    gain_ref[...] = row(10)
    col_ref[...] = jnp.where(own > 0.0, row(8) * SPLIT + row(9) + 1.0, 0.0)

    @pl.loop(0, devices, unroll=4)
    def _(o):
        pick = chosen(rank_ref, o, most)
        at = pl.ds(pl.multiple_of(o * most, 16), most)
        xc_ref[at, :] = jnp.dot(
            jnp.where(pick, 1.0, 0.0).astype(jnp.bfloat16), g_ref[o, 0:rows, :], preferred_element_type=jnp.float32
        ).astype(jnp.bfloat16)
        colc_ref[at, :] = jnp.sum(jnp.where(pick, col_ref[pl.ds(o, 1), :], 0.0), axis=1, keepdims=True) - 1.0

    step = 8 * most

    @pl.loop(0, devices * most // step)
    def _(i):
        at = pl.ds(pl.multiple_of(i * step, 16), step)
        scores = lax.dot_general(
            xc_ref[at, :], cn_ref[...], (((1,), (1,)), ((), ())), preferred_element_type=jnp.float32
        )
        positive = lax.broadcasted_iota(jnp.int32, scores.shape, 1).astype(jnp.float32) == colc_ref[at, :]
        scores = scores - jnp.where(positive, LOGIT_SCALE * MARGIN, 0.0)
        exps = jnp.exp(scores)
        e_ref[at, :] = exps
        sum_ref[at, :] = jnp.sum(exps, axis=1, keepdims=True)
        tgt_ref[at, :] = jnp.sum(jnp.where(positive, scores, 0.0), axis=1, keepdims=True)

    @pl.loop(0, devices, unroll=4)
    def _(o):
        pick = chosen(rank_ref, o, most)
        at = pl.ds(pl.multiple_of(o * most, 16), most)
        part_ref[pl.ds(o, 1), :] = jnp.sum(jnp.where(pick, sum_ref[at, :], 0.0), axis=0, keepdims=True)
        pick_ref[pl.ds(o, 1), :] = jnp.sum(jnp.where(pick, tgt_ref[at, :], 0.0), axis=0, keepdims=True)


def block_scores(most, block, gathered, centers):
    devices, rows, width = gathered.shape
    rows = rows - TAG_ROWS
    capacity = devices * most
    f32 = jnp.float32
    return pl.pallas_call(
        functools.partial(scores_kernel, most),
        out_shape=(
            jax.ShapeDtypeStruct((capacity, width), jnp.bfloat16),
            jax.ShapeDtypeStruct((capacity, centers.shape[0]), f32),
            jax.ShapeDtypeStruct((devices, rows), f32),
            jax.ShapeDtypeStruct((devices, rows), f32),
            jax.ShapeDtypeStruct((devices, rows), f32),
            jax.ShapeDtypeStruct((devices, rows), f32),
            jax.ShapeDtypeStruct((capacity, 1), f32),
        ),
        in_specs=[SMEM, VMEM, VMEM],
        out_specs=(VMEM,) * 7,
        scratch_shapes=[
            pltpu.VMEM(centers.shape, jnp.bfloat16),
            pltpu.VMEM((devices, rows), f32),
            pltpu.VMEM((capacity, 1), f32),
            pltpu.VMEM((capacity, 1), f32),
        ],
        compiler_params=pltpu.CompilerParams(vmem_limit_bytes=VMEM_LIMIT),
        name="block_scores",
    )(block, gathered, centers)


def totals_kernel(depth, part_ref, pick_ref, total_ref, loss_ref, held, landed, send, recv):
    place = Place(depth)
    devices = part_ref.shape[0]
    held[0, 0:devices, :] = part_ref[...]
    held[0, devices : 2 * devices, :] = pick_ref[...]
    barrier = pltpu.get_barrier_semaphore()
    others = [place.sibling(), place.first(), place.second()]
    turns = [
        place.device(lax.rem(place.z + k, depth), place.a, place.b, place.c) for k in range(1, depth)
    ]
    for target in others + turns:
        pl.semaphore_signal(barrier, inc=1, device_id=target, device_id_type=MESH)
    pl.semaphore_wait(barrier, len(others) + len(turns))

    def copy(n, at, target):
        return pltpu.make_async_remote_copy(
            src_ref=held.at[at],
            dst_ref=landed.at[n],
            send_sem=send.at[n],
            recv_sem=recv.at[n],
            device_id=target,
            device_id_type=MESH,
        )

    copies = []
    for n, target in enumerate(others):
        item = copy(n, n, target)
        item.start()
        copies.append(item)
        item.wait_recv()
        held[n + 1] = held[n] + landed[n]
    last = len(others)
    for k, target in enumerate(turns):
        item = copy(last + k, last, target)
        item.start()
        copies.append(item)
    total = held[last]
    for k in range(len(turns)):
        copies[last + k].wait_recv()
        total = total + landed[last + k]
    total_ref[...] = total[0:devices]
    held[last + 1] = total
    mine = pl.ds(place.me, 1)
    loss_ref[...] = jnp.log(held[last + 1, mine, :]) - held[last + 1, pl.ds(place.me + devices, 1), :]
    for item in copies:
        item.wait_send()


def sample_totals(depth, part, pick):
    devices, rows = part.shape
    steps = depth + 2
    return pl.pallas_call(
        functools.partial(totals_kernel, depth),
        out_shape=(
            jax.ShapeDtypeStruct(part.shape, jnp.float32),
            jax.ShapeDtypeStruct((1, rows), jnp.float32),
        ),
        in_specs=[VMEM, VMEM],
        out_specs=(VMEM, VMEM),
        scratch_shapes=[
            pltpu.VMEM((5, 2 * devices, rows), jnp.float32),
            pltpu.VMEM((steps, 2 * devices, rows), jnp.float32),
            pltpu.SemaphoreType.DMA((steps,)),
            pltpu.SemaphoreType.DMA((steps,)),
        ],
        compiler_params=pltpu.CompilerParams(
            collective_id=1, has_side_effects=True, vmem_limit_bytes=VMEM_LIMIT
        ),
        name="sample_totals",
    )(part, pick)


def grads_kernel(most, total_ref, rank_ref, gain_ref, colc_ref, xc_ref, e_ref, c_ref, r_ref, cg_ref, cn_ref, fac_ref, ug_ref, facc_ref, gainc_ref):
    devices, rows = rank_ref.shape
    cn_ref[...] = (center_parts(c_ref)[0].astype(jnp.bfloat16) * LOGIT_SCALE).astype(jnp.bfloat16)
    fac_ref[...] = gain_ref[...] / total_ref[...]
    ug_ref[...] = jnp.zeros_like(ug_ref)

    @pl.loop(0, devices, unroll=4)
    def _(o):
        pick = chosen(rank_ref, o, most)
        at = pl.ds(pl.multiple_of(o * most, 16), most)
        facc_ref[at, :] = jnp.sum(jnp.where(pick, fac_ref[pl.ds(o, 1), :], 0.0), axis=1, keepdims=True)
        gainc_ref[at, :] = jnp.sum(jnp.where(pick, gain_ref[pl.ds(o, 1), :], 0.0), axis=1, keepdims=True)

    group = 8
    step = group * most

    @pl.loop(0, devices // group)
    def _(i):
        at = pl.ds(pl.multiple_of(i * step, 16), step)
        exps = e_ref[at, :]
        positive = lax.broadcasted_iota(jnp.int32, exps.shape, 1).astype(jnp.float32) == colc_ref[at, :]
        weights = exps * facc_ref[at, :] - jnp.where(positive, gainc_ref[at, :], 0.0)
        weights = weights.astype(jnp.bfloat16)
        returned = jnp.dot(weights, cn_ref[...], preferred_element_type=jnp.float32).astype(jnp.bfloat16)
        ug_ref[...] += lax.dot_general(
            weights, xc_ref[at, :], (((0,), (0,)), ((), ())), preferred_element_type=jnp.float32
        )
        for k in range(group):
            o = i * group + k
            pick = jnp.where(chosen(rank_ref, o, most), 1.0, 0.0).astype(jnp.bfloat16)
            r_ref[o] = lax.dot_general(
                pick,
                returned[k * most : (k + 1) * most],
                (((0,), (0,)), ((), ())),
                preferred_element_type=jnp.float32,
            ).astype(jnp.bfloat16)

    unit, lengths = center_parts(c_ref)
    grad = ug_ref[...] * LOGIT_SCALE
    along = jnp.sum(unit * grad, axis=1, keepdims=True)
    cg_ref[...] = ((grad - unit * along) / lengths).astype(jnp.bfloat16)


def block_grads(most, total, rank, gain, colc, xc, exps, centers):
    devices, rows = rank.shape
    capacity, width = xc.shape
    return pl.pallas_call(
        functools.partial(grads_kernel, most),
        out_shape=(
            jax.ShapeDtypeStruct((devices, rows, width), jnp.bfloat16),
            jax.ShapeDtypeStruct(centers.shape, jnp.bfloat16),
        ),
        in_specs=[VMEM] * 7,
        out_specs=(VMEM, VMEM),
        scratch_shapes=[
            pltpu.VMEM(centers.shape, jnp.bfloat16),
            pltpu.VMEM((devices, rows), jnp.float32),
            pltpu.VMEM(centers.shape, jnp.float32),
            pltpu.VMEM((capacity, 1), jnp.float32),
            pltpu.VMEM((capacity, 1), jnp.float32),
        ],
        compiler_params=pltpu.CompilerParams(vmem_limit_bytes=VMEM_LIMIT),
        name="block_grads",
    )(total, rank, gain, colc, xc, exps, centers)


def scatter_kernel(depth, r_ref, x_ref, out_ref, rs, tx2, rx2, tx1, rx1, txz, rxu, rxd, s_sib, v_sib, s2, v2, s1, v1, sz, vu, vd):
    place = Place(depth)
    z, a, b, c = place.z, place.a, place.b, place.c
    f32 = jnp.float32
    greet(place)

    def far_first():
        for r in range(depth - 1, -1, -1):
            for off in offsets_at(r):
                yield off

    def copy(src, dst, send, recv, target):
        return pltpu.make_async_remote_copy(
            src_ref=src, dst_ref=dst, send_sem=send, recv_sem=recv, device_id=target, device_id_type=MESH
        )

    def to_sibling(off, kind):
        o = place.origin(z + off, 1 - b if kind & 1 else b, 1 - a if kind & 2 else a, 1 - c)
        h = lax.div(o, 2)
        return copy(r_ref.at[o], rs.at[h], s_sib.at[h], v_sib.at[h], place.sibling())

    def own_sum(off, kind):
        o = place.origin(z + off, 1 - a if kind & 1 else a, 1 - b if kind & 2 else b, c)
        h = lax.div(o, 2)
        copy(r_ref.at[o], rs.at[h], s_sib.at[h], v_sib.at[h], place.sibling()).wait_recv()
        return r_ref[o].astype(f32) + rs[h].astype(f32)

    def to_second(off, kind):
        slot = (z + off) * 2 + (1 - a if kind & 1 else a)
        return slot, copy(tx2.at[slot], rx2.at[slot], s2.at[slot], v2.at[slot], place.second())

    def to_first(off):
        slot = z + off
        return slot, copy(tx1.at[slot], rx1.at[slot], s1.at[slot], v1.at[slot], place.first())

    def to_up(off):
        slot = z + off
        return slot, copy(txz.at[slot], rxu.at[slot], sz.at[slot], vu.at[slot], place.up())

    def to_down(off):
        slot = z + off
        return slot, copy(txz.at[slot], rxd.at[slot], sz.at[slot], vd.at[slot], place.down())

    order = (3, 2, 1, 0)
    for kind in order:
        for off in far_first():
            place.when(off, lambda: to_sibling(off, kind).start())

    for kind in (3, 2):
        for off in far_first():

            def cross_second():
                total = own_sum(off, kind)
                slot, item = to_second(off, kind)
                tx2[slot] = total.astype(jnp.bfloat16)
                item.start()

            place.when(off, cross_second)
    for off in far_first():

        def cross_first():
            total = own_sum(off, 1)
            far, item = to_second(off, 1)
            item.wait_recv()
            total = total + rx2[far].astype(f32)
            slot, item = to_first(off)
            tx1[slot] = total.astype(jnp.bfloat16)
            item.start()

        place.when(off, cross_first)

    def gathered_sum(off):
        total = own_sum(off, 0)
        far, item = to_second(off, 0)
        item.wait_recv()
        total = total + rx2[far].astype(f32)
        near, item = to_first(off)
        item.wait_recv()
        return total + rx1[near].astype(f32)

    for off in far_first():
        if off == 0:
            continue

        def cross_z():
            slot, item = to_up(off) if off > 0 else to_down(off)
            txz[slot] = gathered_sum(off).astype(jnp.bfloat16)

            @pl.when(z > 0 if off > 0 else z < depth - 1)
            def _():
                item.wait_recv()
                landed = rxu if off > 0 else rxd
                txz[slot] = (txz[slot].astype(f32) + landed[slot].astype(f32)).astype(jnp.bfloat16)

            item.start()

        place.when(off, cross_z)

    out_ref[...] = gathered_sum(0)

    @pl.when(z > 0)
    def _():
        slot, item = to_up(0)
        item.wait_recv()
        out_ref[...] += rxu[slot].astype(f32)

    @pl.when(z < depth - 1)
    def _():
        slot, item = to_down(0)
        item.wait_recv()
        out_ref[...] += rxd[slot].astype(f32)

    widened = x_ref[...].astype(f32)
    lengths = jnp.sqrt(jnp.sum(widened * widened, axis=1, keepdims=True) + EPSILON)
    unit = widened / lengths
    grad = out_ref[...]
    along = jnp.sum(unit * grad, axis=1, keepdims=True)
    out_ref[...] = (grad - unit * along) / lengths

    for off in far_first():

        def drain():
            for kind in order:
                to_sibling(off, kind).wait_send()
            for kind in (3, 2):
                to_second(off, kind)[1].wait_send()
            to_first(off)[1].wait_send()
            if off > 0:
                to_up(off)[1].wait_send()
            if off < 0:
                to_down(off)[1].wait_send()

        place.when(off, drain)


def scatter_rows(depth, returned, features):
    devices, rows, width = returned.shape

    def slots(count):
        return pltpu.VMEM((count, rows, width), jnp.bfloat16)

    def sems(count):
        return pltpu.SemaphoreType.DMA((count,))

    return pl.pallas_call(
        functools.partial(scatter_kernel, depth),
        out_shape=jax.ShapeDtypeStruct((rows, width), jnp.float32),
        in_specs=[VMEM, VMEM],
        out_specs=VMEM,
        scratch_shapes=[
            slots(devices // 2),
            slots(depth * 2),
            slots(depth * 2),
            slots(depth),
            slots(depth),
            slots(depth),
            slots(depth),
            slots(depth),
            sems(devices // 2),
            sems(devices // 2),
            sems(depth * 2),
            sems(depth * 2),
            sems(depth),
            sems(depth),
            sems(depth),
            sems(depth),
            sems(depth),
        ],
        compiler_params=pltpu.CompilerParams(
            collective_id=2, has_side_effects=True, vmem_limit_bytes=VMEM_LIMIT
        ),
        name="scatter_rows",
    )(returned, features)


def on_device_dense(depth, most, features, loss_scale, blocks, label_col, block_slot, centers):
    devices = depth * 8
    rows, width = features.shape
    me = lax.axis_index("dp") * 4 + lax.axis_index("grp")
    block = jnp.sum(jnp.where(block_slot == me, jnp.arange(block_slot.shape[0], dtype=jnp.int32), 0)).reshape(1)
    bf16 = jnp.bfloat16
    tags = jnp.concatenate(
        [
            blocks.T.astype(bf16),
            (label_col // SPLIT).astype(bf16)[None],
            (label_col % SPLIT).astype(bf16)[None],
            loss_scale[None],
        ]
    )
    tags = jnp.pad(tags, ((0, TAG_ROWS - tags.shape[0]), (0, width - rows)))
    gathered = gather_rows(depth, devices, features, tags)
    xc, exps, part, pick, rank, gain, colc = block_scores(most, block, gathered, centers)
    total, loss = sample_totals(depth, part, pick)
    returned, center_grad = block_grads(most, total, rank, gain, colc, xc, exps, centers)
    feature_grad = scatter_rows(depth, returned, features)
    return loss.reshape(-1), feature_grad, center_grad


def chosen_plan(mesh, features, loss_scale, blocks, label_col, block_slot, centers):
    dp_count, groups = mesh.shape["dp"], mesh.shape["grp"]
    rows, picks = blocks.shape
    total = block_slot.shape[0]
    quota = (rows * picks + total - 1) // total
    most = quota + max(1, quota // 2)
    dense = (
        most * 4 >= rows
        and most % 16 == 0
        and rows == 128
        and groups == 4
        and dp_count % 2 == 0
        and total == dp_count * groups
        and total <= 256
        and picks == 8
    )
    args = (features, loss_scale, blocks, label_col, block_slot, centers)
    if dense:
        return on_device_dense(dp_count // 2, most, *args)
    return on_device(*args)


def solution(mesh):
    placed = (
        P(("dp", "grp"), None),
        P(("dp", "grp")),
        P(("dp", "grp"), None),
        P(("dp", "grp")),
        P(),
        P(("dp", "grp"), None),
    )
    return jax.shard_map(
        functools.partial(chosen_plan, mesh),
        mesh=mesh,
        in_specs=placed,
        out_specs=(P(("dp", "grp")), P(("dp", "grp"), None), P(("dp", "grp"), None)),
        check_vma=False,
    )
```

```python
import functools

import jax
import jax.numpy as jnp
from jax import lax
from jax.experimental import pallas as pl
from jax.experimental.pallas import tpu as pltpu
from jax.sharding import PartitionSpec as P

BLOCK = 1024


MARGIN = 0.35
LOGIT_SCALE = 64.0
EPSILON = 1e-06


def normalize(block_w):
    widened = block_w.astype(jnp.float32)
    lengths = jnp.sqrt(jnp.sum(widened * widened, axis=1) + EPSILON)
    unit_rows = widened / lengths[:, None]
    return (unit_rows.astype(jnp.bfloat16), unit_rows, lengths)


def normalize_block(block_w):
    squares = jnp.einsum("re,re->r", block_w, block_w, preferred_element_type=jnp.float32)
    lengths = jnp.sqrt(squares + EPSILON)
    unit_rows = block_w.astype(jnp.float32) / lengths[:, None]
    scaled = unit_rows.astype(jnp.bfloat16) * LOGIT_SCALE
    return (scaled, unit_rows, lengths)


def block_logits(rows_x, scaled_centers, columns):
    width = scaled_centers.shape[0]
    scores = lax.dot_general(
        rows_x, scaled_centers, (((1,), (1,)), ((), ())), preferred_element_type=jnp.float32
    )
    row_iota = jnp.arange(rows_x.shape[0], dtype=jnp.int32)
    target_cols = jnp.where(columns >= 0, columns, width)
    scores = scores.at[row_iota, target_cols].add(-LOGIT_SCALE * MARGIN, mode="drop")
    picked = jnp.where(columns >= 0, scores[row_iota, jnp.maximum(columns, 0)], 0.0)
    return (scores, picked)


def center_terms(exps, factor, columns, gains, rows_x, scaled_centers, unit_rows, lengths):
    width = scaled_centers.shape[0]
    row_iota = jnp.arange(exps.shape[0], dtype=jnp.int32)
    target_cols = jnp.where(columns >= 0, columns, width)
    weights = exps * factor[:, None]
    weights = (
        weights.at[row_iota, target_cols]
        .add(-gains.astype(jnp.float32), mode="drop")
        .astype(jnp.bfloat16)
    )
    returned = jnp.dot(weights, scaled_centers, preferred_element_type=jnp.float32)
    scaled_rows = rows_x * LOGIT_SCALE
    unit_grad = lax.dot_general(
        weights, scaled_rows, (((0,), (0,)), ((), ())), preferred_element_type=jnp.float32
    )
    along_unit = jnp.einsum("re,re->r", unit_rows, unit_grad)
    grad_rows = ((unit_grad - unit_rows * along_unit[:, None]) / lengths[:, None]).astype(
        jnp.bfloat16
    )
    return (returned, grad_rows)


def route_rows(rows_out, gains_out, sample_tags, col_tags):
    return (
        lax.all_to_all(
            lax.all_to_all(rows_out, "dp", split_axis=2, concat_axis=2, tiled=True),
            "grp",
            split_axis=1,
            concat_axis=1,
            tiled=True,
        ),
        lax.all_to_all(
            lax.all_to_all(gains_out, "dp", split_axis=2, concat_axis=2, tiled=True),
            "grp",
            split_axis=1,
            concat_axis=1,
            tiled=True,
        ),
        lax.all_to_all(
            lax.all_to_all(sample_tags, "dp", split_axis=2, concat_axis=2, tiled=True),
            "grp",
            split_axis=1,
            concat_axis=1,
            tiled=True,
        ),
        lax.all_to_all(
            lax.all_to_all(col_tags, "dp", split_axis=2, concat_axis=2, tiled=True),
            "grp",
            split_axis=1,
            concat_axis=1,
            tiled=True,
        ),
    )


def route_grads(returned):
    return lax.all_to_all(
        lax.all_to_all(returned, "dp", split_axis=2, concat_axis=2, tiled=True),
        "grp",
        split_axis=1,
        concat_axis=1,
        tiled=True,
    )


def on_device(features, loss_scale, blocks, label_col, block_slot, centers):
    dp_count = lax.axis_size("dp")
    groups = lax.axis_size("grp")
    sample_count, feature_width = features.shape
    pick_count = blocks.shape[1]
    block_total = block_slot.shape[0]
    per_device = centers.shape[0] // BLOCK
    quota = (sample_count * pick_count + block_total - 1) // block_total
    capacity_most = quota + max(1, quota // 2)
    pair_count = sample_count * pick_count
    layout = (per_device, groups, dp_count, capacity_most)
    slot_total = per_device * groups * dp_count * capacity_most
    capacity = groups * dp_count * capacity_most
    normed_feat, unit_feat, feat_norm = normalize(features)
    flat_blocks = blocks.reshape(-1)
    matches = flat_blocks[:, None] == lax.broadcasted_iota(jnp.int32, (pair_count, block_total), 1)
    slot_ids = jnp.sum(jnp.where(matches, block_slot[None, :], 0), axis=1)
    owner_flat = slot_ids // per_device
    local_block = slot_ids % per_device
    owner_grp = owner_flat % groups
    owner_dp = owner_flat // groups
    sample_of = lax.broadcasted_iota(jnp.int32, (sample_count, pick_count), 0).reshape(-1)
    pick_of = lax.broadcasted_iota(jnp.int32, (sample_count, pick_count), 1).reshape(-1)
    earlier = (flat_blocks[:, None] == flat_blocks[None, :]) & (
        sample_of[None, :] < sample_of[:, None]
    )
    rank_of = jnp.sum(earlier.astype(jnp.int32), axis=1)
    places = ((local_block * groups + owner_grp) * dp_count + owner_dp) * capacity_most + rank_of
    rows_out = (
        jnp.zeros((slot_total, feature_width), jnp.bfloat16)
        .at[places]
        .set(jnp.repeat(normed_feat, pick_count, axis=0))
    )
    gains_out = (
        jnp.zeros((slot_total,), jnp.bfloat16).at[places].set(jnp.repeat(loss_scale, pick_count))
    )
    sample_tags = jnp.full((slot_total,), -1, jnp.int32).at[places].set(sample_of)
    col_values = jnp.where(pick_of == 0, jnp.repeat(label_col, pick_count), -1)
    col_tags = jnp.full((slot_total,), -1, jnp.int32).at[places].set(col_values)
    rows_in, gains_in, samples_in, cols_in = route_rows(
        rows_out.reshape(layout + (feature_width,)),
        gains_out.reshape(layout),
        sample_tags.reshape(layout),
        col_tags.reshape(layout),
    )
    local_idx = 0
    scaled_centers, unit_rows, lengths = normalize_block(centers)
    rows_x = rows_in[local_idx].reshape(capacity, feature_width)
    columns = cols_in[local_idx].reshape(capacity)
    scores, picked = block_logits(rows_x, scaled_centers, columns)
    tag_rows = samples_in[local_idx].reshape(capacity)
    gains = gains_in[local_idx].reshape(capacity)
    local_data = [
        (scores, picked, rows_x, scaled_centers, unit_rows, lengths, gains, tag_rows, columns)
    ]
    entry = local_data[0]
    highest = jnp.max(entry[0], axis=1)
    exps = jnp.exp(entry[0] - highest[:, None])
    exps_list = [exps]
    highs = [highest]
    totals = [jnp.sum(exps, axis=1)]
    picks_list = [entry[1]]
    back_high, back_total, back_pick = (
        lax.all_to_all(
            lax.all_to_all(
                jnp.stack(highs).reshape(layout), "dp", split_axis=2, concat_axis=2, tiled=True
            ),
            "grp",
            split_axis=1,
            concat_axis=1,
            tiled=True,
        ),
        lax.all_to_all(
            lax.all_to_all(
                jnp.stack(totals).reshape(layout), "dp", split_axis=2, concat_axis=2, tiled=True
            ),
            "grp",
            split_axis=1,
            concat_axis=1,
            tiled=True,
        ),
        lax.all_to_all(
            lax.all_to_all(
                jnp.stack(picks_list).reshape(layout), "dp", split_axis=2, concat_axis=2, tiled=True
            ),
            "grp",
            split_axis=1,
            concat_axis=1,
            tiled=True,
        ),
    )
    pair_high = back_high.reshape(-1)[places].reshape(sample_count, pick_count)
    pair_total = back_total.reshape(-1)[places].reshape(sample_count, pick_count)
    pair_pick = back_pick.reshape(-1)[places].reshape(sample_count, pick_count)
    sample_peak = jnp.max(pair_high, axis=1)
    sample_denom = jnp.sum(pair_total * jnp.exp(pair_high - sample_peak[:, None]), axis=1)
    target = jnp.sum(pair_pick, axis=1)
    peak_out = (
        jnp.zeros((slot_total,), jnp.float32).at[places].set(jnp.repeat(sample_peak, pick_count))
    )
    denom_out = (
        jnp.ones((slot_total,), jnp.float32).at[places].set(jnp.repeat(sample_denom, pick_count))
    )
    peak_in, denom_in = (
        lax.all_to_all(
            lax.all_to_all(peak_out.reshape(layout), "dp", split_axis=2, concat_axis=2, tiled=True),
            "grp",
            split_axis=1,
            concat_axis=1,
            tiled=True,
        ),
        lax.all_to_all(
            lax.all_to_all(
                denom_out.reshape(layout), "dp", split_axis=2, concat_axis=2, tiled=True
            ),
            "grp",
            split_axis=1,
            concat_axis=1,
            tiled=True,
        ),
    )
    local_idx = 0
    row_peak = peak_in[local_idx].reshape(capacity)
    row_denom = denom_in[local_idx].reshape(capacity)
    gains = local_data[local_idx][6].astype(jnp.float32)
    factors = [gains * jnp.exp(highs[local_idx] - row_peak) / row_denom]
    loss_out = sample_peak + jnp.log(sample_denom) - target
    local_idx = 0
    entry = local_data[local_idx]
    returned, grad_rows = center_terms(
        exps_list[local_idx],
        factors[local_idx],
        entry[8],
        entry[6],
        entry[2],
        entry[3],
        entry[4],
        entry[5],
    )
    returned_list = [returned]
    back_grads = route_grads(jnp.stack(returned_list).reshape(layout + (feature_width,)))
    pair_grads = back_grads.reshape(slot_total, feature_width)[places].reshape(
        sample_count, pick_count, feature_width
    )
    unit_fgrad = jnp.sum(pair_grads, axis=1)
    along = jnp.sum(unit_feat * unit_fgrad, axis=1, keepdims=True)
    feature_grad = (unit_fgrad - unit_feat * along) / feat_norm[:, None]
    return (loss_out, feature_grad, grad_rows)


MESH = pl.DeviceIdType.MESH
VMEM = pl.BlockSpec(memory_space=pltpu.VMEM)
TAG_ROWS = 16
SPLIT = 32
VMEM_LIMIT = 56 * 1024 * 1024


class Place:
    def __init__(self, depth):
        dp, grp = lax.axis_index("dp"), lax.axis_index("grp")
        self.depth = depth
        self.z, y = lax.div(dp, 2), lax.rem(dp, 2)
        x, self.c = lax.div(grp, 2), lax.rem(grp, 2)
        self.a = y + self.c * (x - y)
        self.b = x + self.c * (y - x)
        self.me = dp * 4 + grp

    def device(self, z, a, b, c):
        y, x = a + c * (b - a), b + c * (a - b)
        return (z * 2 + y, x * 2 + c)

    def origin(self, z, a, b, c):
        dp, grp = self.device(z, a, b, c)
        return dp * 4 + grp

    def up(self):
        return self.device(self.z + 1, self.a, self.b, self.c)

    def down(self):
        return self.device(self.z - 1, self.a, self.b, self.c)

    def first(self):
        return self.device(self.z, 1 - self.a, self.b, self.c)

    def second(self):
        return self.device(self.z, self.a, 1 - self.b, self.c)

    def sibling(self):
        return self.device(self.z, self.b, self.a, 1 - self.c)

    def inside(self, offset):
        if offset == 0:
            return None
        return self.z + offset < self.depth if offset > 0 else self.z + offset >= 0

    def when(self, offset, body):
        if offset == 0:
            body()
        else:
            pl.when(self.inside(offset))(body)


def offsets_at(distance):
    return [0] if distance == 0 else [-distance, distance]


UP, DOWN, FIRST, SECOND, SIB = range(5)
KINDS = 4


def chosen(rank, most):
    shape = (most, rank.shape[1])
    return lax.broadcasted_iota(jnp.int32, shape, 0).astype(jnp.float32) == rank


def one_hot(pick):
    return jnp.where(pick, 1.0, 0.0).astype(jnp.bfloat16)


def positives(columns, width):
    shape = (columns.shape[0], width)
    return lax.broadcasted_iota(jnp.int32, shape, 1).astype(jnp.float32) == columns


def fused_kernel(
    depth, most,
    x_ref, scale_ref, blocks_ref, label_ref, slot_ref, c_ref,
    loss_ref, out_ref, cg_ref,
    g_ref, cn_ref, len_ref, xc_ref, e_ref, w_ref, rank_ref, gain_ref, colc_ref, held, landed,
    r_ref, rs, tx2, rx2, tx1, rx1, txz, rxu, rxd,
    send, recv, s_sum, v_sum, s_sib, v_sib, s2, v2, s1, v1, sz, vu, vd,
):
    f32, bf16 = jnp.float32, jnp.bfloat16
    place = Place(depth)
    z, a, b, c = place.z, place.a, place.b, place.c
    rows, devices = x_ref.shape[0], g_ref.shape[0]
    width = c_ref.shape[0]
    turns = [place.device(lax.rem(z + k, depth), a, b, c) for k in range(1, depth)]
    corner = place.device(z, 1 - a, 1 - b, c)
    partners = [place.sibling(), place.first(), place.second(), corner] + turns
    barrier = pltpu.get_barrier_semaphore()
    for target in partners:
        pl.semaphore_signal(barrier, inc=1, device_id=target, device_id_type=MESH)

    widened = x_ref[...].astype(f32)
    lengths = jnp.sqrt(jnp.sum(widened * widened, axis=1, keepdims=True) + EPSILON)
    g_ref[place.me, 0:rows, :] = (widened / lengths).astype(bf16)
    label = label_ref[...]
    high = lax.div(label, SPLIT)
    named = jnp.concatenate([blocks_ref[...].astype(f32), jnp.zeros((rows, rows - 8), f32)], axis=1)
    tags = jnp.concatenate(
        [
            jnp.transpose(named)[0:8],
            high.astype(f32),
            (label - high * SPLIT).astype(f32),
            scale_ref[...].astype(f32),
            jnp.zeros((TAG_ROWS - 11, rows), f32),
        ],
        axis=0,
    )
    g_ref[place.me, rows : rows + TAG_ROWS, :] = jnp.zeros((TAG_ROWS, x_ref.shape[1]), bf16)
    g_ref[place.me, rows : rows + TAG_ROWS, 0:rows] = tags.astype(bf16)
    slots = slot_ref[...]
    mine = jnp.sum(
        jnp.where(slots == place.me, lax.broadcasted_iota(jnp.int32, slots.shape, 1), 0).astype(f32),
        axis=1,
        keepdims=True,
    )
    pl.semaphore_wait(barrier, len(partners))

    def copy(src, dst, send_sem, recv_sem, target):
        return pltpu.make_async_remote_copy(
            src_ref=src, dst_ref=dst, send_sem=send_sem, recv_sem=recv_sem, device_id=target, device_id_type=MESH
        )

    def package(slot, way, target):
        return copy(g_ref.at[slot], g_ref.at[slot], send.at[way, slot], recv.at[slot], target)

    def arrived(slot):
        package(slot, SIB, place.sibling()).wait_recv()

    def origin(cls, kind, level):
        if cls == 0:
            return place.origin(level, 1 - a if kind & 1 else a, 1 - b if kind & 2 else b, c)
        return place.origin(level, 1 - b if kind & 1 else b, 1 - a if kind & 2 else a, 1 - c)

    def handle(off, kind, act, wait):
        def body():
            slot = origin(0, kind, z + off)
            if wait and (off != 0 or kind != 0):
                arrived(slot)
            if kind == 0 and off <= 0:
                pl.when(z < depth - 1)(lambda: act(package(slot, UP, place.up())))
            if kind == 0 and off >= 0:
                pl.when(z > 0)(lambda: act(package(slot, DOWN, place.down())))
            if kind < 2:
                act(package(slot, SECOND, place.second()))
            if kind < 1:
                act(package(slot, FIRST, place.first()))
            act(package(slot, SIB, place.sibling()))

        place.when(off, body)

    def events(r):
        if r < depth:
            for off in offsets_at(r):
                yield off, 0
        if 1 <= r <= depth:
            for off in offsets_at(r - 1):
                yield off, 1
                yield off, 2
        if 2 <= r <= depth + 1:
            for off in offsets_at(r - 2):
                yield off, 3

    def span(j, level=None):
        if level is None:
            return slice(j * depth * most, (j + 1) * depth * most)
        return slice((j * depth + level) * most, (j * depth + level + 1) * most)

    def stacked(parts):
        return jnp.concatenate(parts, axis=0)

    def score(cls, kind):
        j = cls * KINDS + kind
        levels = range(depth)
        where_from = [origin(cls, kind, level) for level in levels]
        if cls == 1:
            for o in where_from:
                arrived(o)
        tagged = [g_ref[o, rows : rows + TAG_ROWS, 0:rows].astype(f32) for o in where_from]
        hits = [jnp.where(t[0:8] == mine, 1.0, 0.0) for t in tagged]
        wanted = stacked([jnp.sum(hit, axis=0, keepdims=True) for hit in hits])
        shape = (rows, rows)
        earlier = lax.broadcasted_iota(jnp.int32, shape, 0) < lax.broadcasted_iota(jnp.int32, shape, 1)
        padded = stacked([wanted, jnp.zeros((16 - depth % 16, rows), f32)]).astype(bf16)
        ahead = jnp.dot(padded, one_hot(earlier), preferred_element_type=f32)[0:depth]
        rank = jnp.where(wanted > 0.0, ahead, -1.0)
        picks, columns = [], []
        for level in levels:
            p = j * depth + level
            rank_ref[p : p + 1, :] = rank[level : level + 1]
            gain_ref[p : p + 1, :] = tagged[level][10:11]
            pick = chosen(rank[level : level + 1], most)
            column = jnp.where(hits[level][0:1] > 0.0, tagged[level][8:9] * SPLIT + tagged[level][9:10] + 1.0, 0.0)
            picks.append(pick)
            columns.append(jnp.sum(jnp.where(pick, column, 0.0), axis=1, keepdims=True) - 1.0)
            xc_ref[span(j, level), :] = jnp.dot(
                one_hot(pick), g_ref[where_from[level], 0:rows, :], preferred_element_type=f32
            ).astype(bf16)
        columns = stacked(columns)
        colc_ref[span(j), :] = columns
        scores = lax.dot_general(
            xc_ref[span(j), :], cn_ref[...], (((1,), (1,)), ((), ())), preferred_element_type=f32
        )
        positive = positives(columns, width)
        scores = scores - jnp.where(positive, LOGIT_SCALE * MARGIN, 0.0)
        exps = jnp.exp(scores)
        e_ref[span(j), :] = exps
        sums = jnp.sum(exps, axis=1, keepdims=True)
        target = jnp.sum(jnp.where(positive, scores, 0.0), axis=1, keepdims=True)
        for level in levels:
            at = slice(level * most, (level + 1) * most)
            o = where_from[level]
            held[0, pl.ds(o, 1), :] = jnp.sum(jnp.where(picks[level], sums[at], 0.0), axis=0, keepdims=True)
            held[0, pl.ds(o + devices, 1), :] = jnp.sum(
                jnp.where(picks[level], target[at], 0.0), axis=0, keepdims=True
            )

    start = lambda item: item.start()
    for r in range(depth + 2):
        for off, kind in events(r):
            handle(off, kind, start, True)
        if r == 0:
            centers = c_ref[...].astype(f32)
            center_len = jnp.sqrt(jnp.sum(centers * centers, axis=1, keepdims=True) + EPSILON)
            len_ref[...] = center_len
            cn_ref[...] = ((centers / center_len).astype(bf16) * LOGIT_SCALE).astype(bf16)
        if r == depth - 1:
            score(0, 0)
            score(1, 0)
        if r == depth:
            score(0, 1)
    for cls, kind in ((1, 1), (0, 2), (1, 2), (0, 3), (1, 3)):
        score(cls, kind)

    started = []

    def share(n, src, target):
        item = copy(held.at[src], landed.at[n], s_sum.at[n], v_sum.at[n], target)
        item.start()
        started.append(item)

    share(0, 0, partners[0])
    started[0].wait_recv()
    held[1] = held[0] + landed[0]
    for n in (1, 2, 3):
        share(n, 1, partners[n])
    for n in (1, 2, 3):
        started[n].wait_recv()
    held[2] = (held[1] + landed[1]) + (landed[2] + landed[3])
    for n in range(4, len(partners)):
        share(n, 2, partners[n])
    for n in range(4, len(partners)):
        started[n].wait_recv()
    total = held[2]
    for n in range(4, len(partners)):
        total = total + landed[n]
    held[3] = total

    def grads(cls, kind):
        j = cls * KINDS + kind
        picks, factors, gains = [], [], []
        for level in range(depth):
            p = j * depth + level
            pick = chosen(rank_ref[p : p + 1, :], most)
            gain = gain_ref[p : p + 1, :]
            factor = gain / held[3, pl.ds(origin(cls, kind, level), 1), :]
            picks.append(pick)
            factors.append(jnp.sum(jnp.where(pick, factor, 0.0), axis=1, keepdims=True))
            gains.append(jnp.sum(jnp.where(pick, gain, 0.0), axis=1, keepdims=True))
        positive = positives(colc_ref[span(j), :], width)
        weights = e_ref[span(j), :] * stacked(factors) - jnp.where(positive, stacked(gains), 0.0)
        weights = weights.astype(bf16)
        w_ref[span(j), :] = weights
        returned = jnp.dot(weights, cn_ref[...], preferred_element_type=f32).astype(bf16)
        for level in range(depth):
            r_ref[j * depth + level] = lax.dot_general(
                one_hot(picks[level]),
                returned[level * most : (level + 1) * most],
                (((0,), (0,)), ((), ())),
                preferred_element_type=f32,
            ).astype(bf16)

    def center_rows(n, pieces):
        size = width // pieces
        at = slice(n * size, (n + 1) * size)
        grad = LOGIT_SCALE * lax.dot_general(
            w_ref[:, at], xc_ref[...], (((0,), (0,)), ((), ())), preferred_element_type=f32
        )
        lens = len_ref[at, :]
        unit = c_ref[at, :].astype(f32) / lens
        along = jnp.sum(unit * grad, axis=1, keepdims=True)
        cg_ref[at, :] = ((grad - unit * along) / lens).astype(bf16)

    def to_sibling(kind, level):
        slot = kind * depth + level
        return copy(
            r_ref.at[(KINDS + kind) * depth + level], rs.at[slot], s_sib.at[slot], v_sib.at[slot], place.sibling()
        )

    def to_second(kind, level):
        slot = (kind & 1) * depth + level
        return copy(tx2.at[slot], rx2.at[slot], s2.at[slot], v2.at[slot], place.second())

    def to_first(level):
        return copy(tx1.at[level], rx1.at[level], s1.at[level], v1.at[level], place.first())

    def to_up(slot):
        return copy(txz.at[slot], rxu.at[slot], sz.at[slot], vu.at[slot], place.up())

    def to_down(slot):
        return copy(txz.at[slot], rxd.at[slot], sz.at[slot], vd.at[slot], place.down())

    def own_sum(kind, level):
        to_sibling(kind, level).wait_recv()
        slot = kind * depth + level
        return r_ref[slot].astype(f32) + rs[slot].astype(f32)

    for kind in (3, 2):
        grads(1, kind)
        for level in range(depth):
            to_sibling(kind, level).start()
        grads(0, kind)
        for level in range(depth):
            tx2[(kind & 1) * depth + level] = own_sum(kind, level).astype(bf16)
            to_second(kind, level).start()
    for kind in (1, 0):
        grads(1, kind)
        for level in range(depth):
            to_sibling(kind, level).start()
    grads(0, 1)
    grads(0, 0)
    center_rows(0, 4)
    for level in range(depth):
        total = own_sum(1, level)
        to_second(3, level).wait_recv()
        tx1[level] = (total + rx2[depth + level].astype(f32)).astype(bf16)
        to_first(level).start()
    center_rows(1, 4)

    def gathered_sum(level):
        total = rs[level].astype(f32) + r_ref[level].astype(f32)
        return total + rx2[level].astype(f32) + rx1[level].astype(f32)

    for level in range(depth):
        to_sibling(0, level).wait_recv()
        to_second(2, level).wait_recv()
        to_first(level).wait_recv()

    for r in range(depth - 1, 0, -1):
        for off in offsets_at(r):

            def cross_z():
                slot = z + off
                item = to_up(slot) if off > 0 else to_down(slot)
                txz[slot] = gathered_sum(slot).astype(bf16)

                @pl.when(z > 0 if off > 0 else z < depth - 1)
                def _():
                    item.wait_recv()
                    arriving = rxu if off > 0 else rxd
                    txz[slot] = (txz[slot].astype(f32) + arriving[slot].astype(f32)).astype(bf16)

                item.start()

            place.when(off, cross_z)
    center_rows(2, 4)
    center_rows(3, 4)

    out_ref[...] = gathered_sum(z)

    @pl.when(z > 0)
    def _():
        to_up(z).wait_recv()
        out_ref[...] += rxu[z].astype(f32)

    @pl.when(z < depth - 1)
    def _():
        to_down(z).wait_recv()
        out_ref[...] += rxd[z].astype(f32)

    widened = x_ref[...].astype(f32)
    lengths = jnp.sqrt(jnp.sum(widened * widened, axis=1, keepdims=True) + EPSILON)
    unit = widened / lengths
    grad = out_ref[...]
    along = jnp.sum(unit * grad, axis=1, keepdims=True)
    out_ref[...] = (grad - unit * along) / lengths
    loss_ref[...] = jnp.log(held[3, pl.ds(place.me, 1), :]) - held[3, pl.ds(place.me + devices, 1), :]

    for r in range(depth + 2):
        for off, kind in events(r):
            handle(off, kind, lambda item: item.wait_send(), False)
    for item in started:
        item.wait_send()
    for level in range(depth):
        for kind in range(KINDS):
            to_sibling(kind, level).wait_send()
        for kind in (3, 2):
            to_second(kind, level).wait_send()
        to_first(level).wait_send()
    for r in range(1, depth):
        for off in offsets_at(r):
            place.when(off, lambda: (to_up if off > 0 else to_down)(z + off).wait_send())


def on_device_dense(depth, most, features, loss_scale, blocks, label_col, block_slot, centers):
    devices = depth * 8
    rows, width = features.shape
    capacity = devices * most
    f32, bf16 = jnp.float32, jnp.bfloat16

    def slots(count):
        return pltpu.VMEM((count, rows, width), bf16)

    def sems(*shape):
        return pltpu.SemaphoreType.DMA(shape)

    loss, feature_grad, center_grad = pl.pallas_call(
        functools.partial(fused_kernel, depth, most),
        out_shape=(
            jax.ShapeDtypeStruct((1, rows), f32),
            jax.ShapeDtypeStruct((rows, width), f32),
            jax.ShapeDtypeStruct(centers.shape, bf16),
        ),
        in_specs=[VMEM] * 6,
        out_specs=(VMEM,) * 3,
        scratch_shapes=[
            pltpu.VMEM((devices, rows + TAG_ROWS, width), bf16),
            pltpu.VMEM(centers.shape, bf16),
            pltpu.VMEM((centers.shape[0], 1), f32),
            pltpu.VMEM((capacity, width), bf16),
            pltpu.VMEM((capacity, centers.shape[0]), f32),
            pltpu.VMEM((capacity, centers.shape[0]), bf16),
            pltpu.VMEM((devices, rows), f32),
            pltpu.VMEM((devices, rows), f32),
            pltpu.VMEM((capacity, 1), f32),
            pltpu.VMEM((4, 2 * devices, rows), f32),
            pltpu.VMEM((depth + 3, 2 * devices, rows), f32),
            slots(devices),
            slots(devices // 2),
            slots(depth * 2),
            slots(depth * 2),
            slots(depth),
            slots(depth),
            slots(depth),
            slots(depth),
            slots(depth),
            sems(5, devices),
            sems(devices),
            sems(depth + 3),
            sems(depth + 3),
            sems(devices // 2),
            sems(devices // 2),
            sems(depth * 2),
            sems(depth * 2),
            sems(depth),
            sems(depth),
            sems(depth),
            sems(depth),
            sems(depth),
        ],
        compiler_params=pltpu.CompilerParams(
            collective_id=0, has_side_effects=True, vmem_limit_bytes=VMEM_LIMIT
        ),
        name="partial_softmax",
    )(features, loss_scale[None], blocks, label_col[None], block_slot[None], centers)
    return loss.reshape(-1), feature_grad, center_grad


def chosen_plan(mesh, features, loss_scale, blocks, label_col, block_slot, centers):
    dp_count, groups = mesh.shape["dp"], mesh.shape["grp"]
    rows, picks = blocks.shape
    total = block_slot.shape[0]
    quota = (rows * picks + total - 1) // total
    most = quota + max(1, quota // 2)
    dense = (
        most * 4 >= rows
        and most % 16 == 0
        and rows == 128
        and groups == 4
        and dp_count % 2 == 0
        and total == dp_count * groups
        and total <= 256
        and picks == 8
    )
    args = (features, loss_scale, blocks, label_col, block_slot, centers)
    if dense:
        return on_device_dense(dp_count // 2, most, *args)
    return on_device(*args)


def solution(mesh):
    placed = (
        P(("dp", "grp"), None),
        P(("dp", "grp")),
        P(("dp", "grp"), None),
        P(("dp", "grp")),
        P(),
        P(("dp", "grp"), None),
    )
    return jax.shard_map(
        functools.partial(chosen_plan, mesh),
        mesh=mesh,
        in_specs=placed,
        out_specs=(P(("dp", "grp")), P(("dp", "grp"), None), P(("dp", "grp"), None)),
        check_vma=False,
    )
```

```python
import functools

import jax
import jax.numpy as jnp
from jax import lax
from jax.experimental import pallas as pl
from jax.experimental.pallas import tpu as pltpu
from jax.sharding import PartitionSpec as P

BLOCK = 1024


MARGIN = 0.35
LOGIT_SCALE = 64.0
EPSILON = 1e-06


def normalize(block_w):
    widened = block_w.astype(jnp.float32)
    lengths = jnp.sqrt(jnp.sum(widened * widened, axis=1) + EPSILON)
    unit_rows = widened / lengths[:, None]
    return (unit_rows.astype(jnp.bfloat16), unit_rows, lengths)


def normalize_block(block_w):
    squares = jnp.einsum("re,re->r", block_w, block_w, preferred_element_type=jnp.float32)
    lengths = jnp.sqrt(squares + EPSILON)
    unit_rows = block_w.astype(jnp.float32) / lengths[:, None]
    scaled = unit_rows.astype(jnp.bfloat16) * LOGIT_SCALE
    return (scaled, unit_rows, lengths)


def block_logits(rows_x, scaled_centers, columns):
    width = scaled_centers.shape[0]
    scores = lax.dot_general(
        rows_x, scaled_centers, (((1,), (1,)), ((), ())), preferred_element_type=jnp.float32
    )
    row_iota = jnp.arange(rows_x.shape[0], dtype=jnp.int32)
    target_cols = jnp.where(columns >= 0, columns, width)
    scores = scores.at[row_iota, target_cols].add(-LOGIT_SCALE * MARGIN, mode="drop")
    picked = jnp.where(columns >= 0, scores[row_iota, jnp.maximum(columns, 0)], 0.0)
    return (scores, picked)


def center_terms(exps, factor, columns, gains, rows_x, scaled_centers, unit_rows, lengths):
    width = scaled_centers.shape[0]
    row_iota = jnp.arange(exps.shape[0], dtype=jnp.int32)
    target_cols = jnp.where(columns >= 0, columns, width)
    weights = exps * factor[:, None]
    weights = (
        weights.at[row_iota, target_cols]
        .add(-gains.astype(jnp.float32), mode="drop")
        .astype(jnp.bfloat16)
    )
    returned = jnp.dot(weights, scaled_centers, preferred_element_type=jnp.float32)
    scaled_rows = rows_x * LOGIT_SCALE
    unit_grad = lax.dot_general(
        weights, scaled_rows, (((0,), (0,)), ((), ())), preferred_element_type=jnp.float32
    )
    along_unit = jnp.einsum("re,re->r", unit_rows, unit_grad)
    grad_rows = ((unit_grad - unit_rows * along_unit[:, None]) / lengths[:, None]).astype(
        jnp.bfloat16
    )
    return (returned, grad_rows)


def route_rows(rows_out, gains_out, sample_tags, col_tags):
    return (
        lax.all_to_all(
            lax.all_to_all(rows_out, "dp", split_axis=2, concat_axis=2, tiled=True),
            "grp",
            split_axis=1,
            concat_axis=1,
            tiled=True,
        ),
        lax.all_to_all(
            lax.all_to_all(gains_out, "dp", split_axis=2, concat_axis=2, tiled=True),
            "grp",
            split_axis=1,
            concat_axis=1,
            tiled=True,
        ),
        lax.all_to_all(
            lax.all_to_all(sample_tags, "dp", split_axis=2, concat_axis=2, tiled=True),
            "grp",
            split_axis=1,
            concat_axis=1,
            tiled=True,
        ),
        lax.all_to_all(
            lax.all_to_all(col_tags, "dp", split_axis=2, concat_axis=2, tiled=True),
            "grp",
            split_axis=1,
            concat_axis=1,
            tiled=True,
        ),
    )


def route_grads(returned):
    return lax.all_to_all(
        lax.all_to_all(returned, "dp", split_axis=2, concat_axis=2, tiled=True),
        "grp",
        split_axis=1,
        concat_axis=1,
        tiled=True,
    )


def on_device(features, loss_scale, blocks, label_col, block_slot, centers):
    dp_count = lax.axis_size("dp")
    groups = lax.axis_size("grp")
    sample_count, feature_width = features.shape
    pick_count = blocks.shape[1]
    block_total = block_slot.shape[0]
    per_device = centers.shape[0] // BLOCK
    quota = (sample_count * pick_count + block_total - 1) // block_total
    capacity_most = quota + max(1, quota // 2)
    pair_count = sample_count * pick_count
    layout = (per_device, groups, dp_count, capacity_most)
    slot_total = per_device * groups * dp_count * capacity_most
    capacity = groups * dp_count * capacity_most
    normed_feat, unit_feat, feat_norm = normalize(features)
    flat_blocks = blocks.reshape(-1)
    matches = flat_blocks[:, None] == lax.broadcasted_iota(jnp.int32, (pair_count, block_total), 1)
    slot_ids = jnp.sum(jnp.where(matches, block_slot[None, :], 0), axis=1)
    owner_flat = slot_ids // per_device
    local_block = slot_ids % per_device
    owner_grp = owner_flat % groups
    owner_dp = owner_flat // groups
    sample_of = lax.broadcasted_iota(jnp.int32, (sample_count, pick_count), 0).reshape(-1)
    pick_of = lax.broadcasted_iota(jnp.int32, (sample_count, pick_count), 1).reshape(-1)
    earlier = (flat_blocks[:, None] == flat_blocks[None, :]) & (
        sample_of[None, :] < sample_of[:, None]
    )
    rank_of = jnp.sum(earlier.astype(jnp.int32), axis=1)
    places = ((local_block * groups + owner_grp) * dp_count + owner_dp) * capacity_most + rank_of
    rows_out = (
        jnp.zeros((slot_total, feature_width), jnp.bfloat16)
        .at[places]
        .set(jnp.repeat(normed_feat, pick_count, axis=0))
    )
    gains_out = (
        jnp.zeros((slot_total,), jnp.bfloat16).at[places].set(jnp.repeat(loss_scale, pick_count))
    )
    sample_tags = jnp.full((slot_total,), -1, jnp.int32).at[places].set(sample_of)
    col_values = jnp.where(pick_of == 0, jnp.repeat(label_col, pick_count), -1)
    col_tags = jnp.full((slot_total,), -1, jnp.int32).at[places].set(col_values)
    rows_in, gains_in, samples_in, cols_in = route_rows(
        rows_out.reshape(layout + (feature_width,)),
        gains_out.reshape(layout),
        sample_tags.reshape(layout),
        col_tags.reshape(layout),
    )
    local_idx = 0
    scaled_centers, unit_rows, lengths = normalize_block(centers)
    rows_x = rows_in[local_idx].reshape(capacity, feature_width)
    columns = cols_in[local_idx].reshape(capacity)
    scores, picked = block_logits(rows_x, scaled_centers, columns)
    tag_rows = samples_in[local_idx].reshape(capacity)
    gains = gains_in[local_idx].reshape(capacity)
    local_data = [
        (scores, picked, rows_x, scaled_centers, unit_rows, lengths, gains, tag_rows, columns)
    ]
    entry = local_data[0]
    highest = jnp.max(entry[0], axis=1)
    exps = jnp.exp(entry[0] - highest[:, None])
    exps_list = [exps]
    highs = [highest]
    totals = [jnp.sum(exps, axis=1)]
    picks_list = [entry[1]]
    back_high, back_total, back_pick = (
        lax.all_to_all(
            lax.all_to_all(
                jnp.stack(highs).reshape(layout), "dp", split_axis=2, concat_axis=2, tiled=True
            ),
            "grp",
            split_axis=1,
            concat_axis=1,
            tiled=True,
        ),
        lax.all_to_all(
            lax.all_to_all(
                jnp.stack(totals).reshape(layout), "dp", split_axis=2, concat_axis=2, tiled=True
            ),
            "grp",
            split_axis=1,
            concat_axis=1,
            tiled=True,
        ),
        lax.all_to_all(
            lax.all_to_all(
                jnp.stack(picks_list).reshape(layout), "dp", split_axis=2, concat_axis=2, tiled=True
            ),
            "grp",
            split_axis=1,
            concat_axis=1,
            tiled=True,
        ),
    )
    pair_high = back_high.reshape(-1)[places].reshape(sample_count, pick_count)
    pair_total = back_total.reshape(-1)[places].reshape(sample_count, pick_count)
    pair_pick = back_pick.reshape(-1)[places].reshape(sample_count, pick_count)
    sample_peak = jnp.max(pair_high, axis=1)
    sample_denom = jnp.sum(pair_total * jnp.exp(pair_high - sample_peak[:, None]), axis=1)
    target = jnp.sum(pair_pick, axis=1)
    peak_out = (
        jnp.zeros((slot_total,), jnp.float32).at[places].set(jnp.repeat(sample_peak, pick_count))
    )
    denom_out = (
        jnp.ones((slot_total,), jnp.float32).at[places].set(jnp.repeat(sample_denom, pick_count))
    )
    peak_in, denom_in = (
        lax.all_to_all(
            lax.all_to_all(peak_out.reshape(layout), "dp", split_axis=2, concat_axis=2, tiled=True),
            "grp",
            split_axis=1,
            concat_axis=1,
            tiled=True,
        ),
        lax.all_to_all(
            lax.all_to_all(
                denom_out.reshape(layout), "dp", split_axis=2, concat_axis=2, tiled=True
            ),
            "grp",
            split_axis=1,
            concat_axis=1,
            tiled=True,
        ),
    )
    local_idx = 0
    row_peak = peak_in[local_idx].reshape(capacity)
    row_denom = denom_in[local_idx].reshape(capacity)
    gains = local_data[local_idx][6].astype(jnp.float32)
    factors = [gains * jnp.exp(highs[local_idx] - row_peak) / row_denom]
    loss_out = sample_peak + jnp.log(sample_denom) - target
    local_idx = 0
    entry = local_data[local_idx]
    returned, grad_rows = center_terms(
        exps_list[local_idx],
        factors[local_idx],
        entry[8],
        entry[6],
        entry[2],
        entry[3],
        entry[4],
        entry[5],
    )
    returned_list = [returned]
    back_grads = route_grads(jnp.stack(returned_list).reshape(layout + (feature_width,)))
    pair_grads = back_grads.reshape(slot_total, feature_width)[places].reshape(
        sample_count, pick_count, feature_width
    )
    unit_fgrad = jnp.sum(pair_grads, axis=1)
    along = jnp.sum(unit_feat * unit_fgrad, axis=1, keepdims=True)
    feature_grad = (unit_fgrad - unit_feat * along) / feat_norm[:, None]
    return (loss_out, feature_grad, grad_rows)


MESH = pl.DeviceIdType.MESH
VMEM = pl.BlockSpec(memory_space=pltpu.VMEM)
TAG_ROWS = 16
SPLIT = 32
VMEM_LIMIT = 56 * 1024 * 1024


class Place:
    def __init__(self, depth):
        dp, grp = lax.axis_index("dp"), lax.axis_index("grp")
        self.depth = depth
        self.z, y = lax.div(dp, 2), lax.rem(dp, 2)
        x, self.c = lax.div(grp, 2), lax.rem(grp, 2)
        self.a = y + self.c * (x - y)
        self.b = x + self.c * (y - x)
        self.me = dp * 4 + grp

    def device(self, z, a, b, c):
        y, x = a + c * (b - a), b + c * (a - b)
        return (z * 2 + y, x * 2 + c)

    def origin(self, z, a, b, c):
        dp, grp = self.device(z, a, b, c)
        return dp * 4 + grp

    def up(self):
        return self.device(self.z + 1, self.a, self.b, self.c)

    def down(self):
        return self.device(self.z - 1, self.a, self.b, self.c)

    def first(self):
        return self.device(self.z, 1 - self.a, self.b, self.c)

    def second(self):
        return self.device(self.z, self.a, 1 - self.b, self.c)

    def sibling(self):
        return self.device(self.z, self.b, self.a, 1 - self.c)

    def inside(self, offset):
        if offset == 0:
            return None
        return self.z + offset < self.depth if offset > 0 else self.z + offset >= 0

    def when(self, offset, body):
        if offset == 0:
            body()
        else:
            pl.when(self.inside(offset))(body)


def offsets_at(distance):
    return [0] if distance == 0 else [-distance, distance]


UP, DOWN, FIRST, SECOND, SIB = range(5)
KINDS = 4


def chosen(rank, most):
    shape = (most, rank.shape[1])
    return lax.broadcasted_iota(jnp.int32, shape, 0).astype(jnp.float32) == rank


def one_hot(pick):
    return jnp.where(pick, 1.0, 0.0).astype(jnp.bfloat16)


def positives(columns, width):
    shape = (columns.shape[0], width)
    return lax.broadcasted_iota(jnp.int32, shape, 1).astype(jnp.float32) == columns


def fused_kernel(
    depth, most,
    x_ref, scale_ref, blocks_ref, label_ref, slot_ref, c_ref,
    loss_ref, out_ref, cg_ref,
    g_ref, cn_ref, cnt_ref, len_ref, xc_ref, e_ref, w_ref, rank_ref, gain_ref, colc_ref, held, landed,
    r_ref, rs, tx2, rx2, tx1, rx1, txz, rxu, rxd,
    send, recv, s_sum, v_sum, s_sib, v_sib, s2, v2, s1, v1, sz, vu, vd,
):
    f32, bf16 = jnp.float32, jnp.bfloat16
    place = Place(depth)
    z, a, b, c = place.z, place.a, place.b, place.c
    rows, devices = x_ref.shape[0], g_ref.shape[0]
    width = c_ref.shape[0]
    turns = [place.device(lax.rem(z + k, depth), a, b, c) for k in range(1, depth)]
    corner = place.device(z, 1 - a, 1 - b, c)
    partners = [place.sibling(), place.first(), place.second(), corner] + turns
    barrier = pltpu.get_barrier_semaphore()
    for target in partners:
        pl.semaphore_signal(barrier, inc=1, device_id=target, device_id_type=MESH)

    widened = x_ref[...].astype(f32)
    lengths = jnp.sqrt(jnp.sum(widened * widened, axis=1, keepdims=True) + EPSILON)
    g_ref[place.me, 0:rows, :] = (widened / lengths).astype(bf16)
    label = label_ref[...]
    high = lax.div(label, SPLIT)
    named = jnp.concatenate([blocks_ref[...].astype(f32), jnp.zeros((rows, rows - 8), f32)], axis=1)
    tags = jnp.concatenate(
        [
            jnp.transpose(named)[0:8],
            high.astype(f32),
            (label - high * SPLIT).astype(f32),
            scale_ref[...].astype(f32),
            jnp.zeros((TAG_ROWS - 11, rows), f32),
        ],
        axis=0,
    )
    g_ref[place.me, rows : rows + TAG_ROWS, :] = jnp.zeros((TAG_ROWS, x_ref.shape[1]), bf16)
    g_ref[place.me, rows : rows + TAG_ROWS, 0:rows] = tags.astype(bf16)
    slots = slot_ref[...]
    mine = jnp.sum(
        jnp.where(slots == place.me, lax.broadcasted_iota(jnp.int32, slots.shape, 1), 0).astype(f32),
        axis=1,
        keepdims=True,
    )
    pl.semaphore_wait(barrier, len(partners))

    def copy(src, dst, send_sem, recv_sem, target):
        return pltpu.make_async_remote_copy(
            src_ref=src, dst_ref=dst, send_sem=send_sem, recv_sem=recv_sem, device_id=target, device_id_type=MESH
        )

    def package(slot, way, target):
        return copy(g_ref.at[slot], g_ref.at[slot], send.at[way, slot], recv.at[slot], target)

    def arrived(slot):
        package(slot, SIB, place.sibling()).wait_recv()

    def origin(cls, kind, level):
        if cls == 0:
            return place.origin(level, 1 - a if kind & 1 else a, 1 - b if kind & 2 else b, c)
        return place.origin(level, 1 - b if kind & 1 else b, 1 - a if kind & 2 else a, 1 - c)

    def handle(off, kind, act, wait):
        def body():
            slot = origin(0, kind, z + off)
            if wait and (off != 0 or kind != 0):
                arrived(slot)
            if kind == 0 and off <= 0:
                pl.when(z < depth - 1)(lambda: act(package(slot, UP, place.up())))
            if kind == 0 and off >= 0:
                pl.when(z > 0)(lambda: act(package(slot, DOWN, place.down())))
            if kind < 2:
                act(package(slot, SECOND, place.second()))
            if kind < 1:
                act(package(slot, FIRST, place.first()))
            act(package(slot, SIB, place.sibling()))

        place.when(off, body)

    def events(r):
        if r < depth:
            for off in offsets_at(r):
                yield off, 0
        if 1 <= r <= depth:
            for off in offsets_at(r - 1):
                yield off, 1
                yield off, 2
        if 2 <= r <= depth + 1:
            for off in offsets_at(r - 2):
                yield off, 3

    def span(j, level=None):
        if level is None:
            return slice(j * depth * most, (j + 1) * depth * most)
        return slice((j * depth + level) * most, (j * depth + level + 1) * most)

    def stacked(parts):
        return jnp.concatenate(parts, axis=0)

    def score(cls, kind):
        j = cls * KINDS + kind
        levels = range(depth)
        where_from = [origin(cls, kind, level) for level in levels]
        if cls == 1:
            for o in where_from:
                arrived(o)
        tagged = [g_ref[o, rows : rows + TAG_ROWS, 0:rows].astype(f32) for o in where_from]
        hits = [jnp.where(t[0:8] == mine, 1.0, 0.0) for t in tagged]
        wanted = stacked([jnp.sum(hit, axis=0, keepdims=True) for hit in hits])
        shape = (rows, rows)
        earlier = lax.broadcasted_iota(jnp.int32, shape, 0) < lax.broadcasted_iota(jnp.int32, shape, 1)
        padded = stacked([wanted, jnp.zeros((16 - depth % 16, rows), f32)]).astype(bf16)
        ahead = jnp.dot(padded, one_hot(earlier), preferred_element_type=f32)[0:depth]
        rank = jnp.where(wanted > 0.0, ahead, -1.0)
        picks, columns = [], []
        for level in levels:
            p = j * depth + level
            rank_ref[p : p + 1, :] = rank[level : level + 1]
            gain_ref[p : p + 1, :] = tagged[level][10:11]
            pick = chosen(rank[level : level + 1], most)
            column = jnp.where(hits[level][0:1] > 0.0, tagged[level][8:9] * SPLIT + tagged[level][9:10] + 1.0, 0.0)
            picks.append(pick)
            columns.append(jnp.sum(jnp.where(pick, column, 0.0), axis=1, keepdims=True) - 1.0)
            xc_ref[span(j, level), :] = jnp.dot(
                one_hot(pick), g_ref[where_from[level], 0:rows, :], preferred_element_type=f32
            ).astype(bf16)
        columns = stacked(columns)
        colc_ref[span(j), :] = columns
        scores = lax.dot_general(
            xc_ref[span(j), :], cnt_ref[...], (((1,), (0,)), ((), ())), preferred_element_type=f32
        )
        positive = positives(columns, width)
        scores = scores - jnp.where(positive, LOGIT_SCALE * MARGIN, 0.0)
        exps = jnp.exp(scores)
        e_ref[span(j), :] = exps
        sums = jnp.sum(exps, axis=1, keepdims=True)
        target = jnp.sum(jnp.where(positive, scores, 0.0), axis=1, keepdims=True)
        for level in levels:
            at = slice(level * most, (level + 1) * most)
            o = where_from[level]
            held[0, pl.ds(o, 1), :] = jnp.sum(jnp.where(picks[level], sums[at], 0.0), axis=0, keepdims=True)
            held[0, pl.ds(o + devices, 1), :] = jnp.sum(
                jnp.where(picks[level], target[at], 0.0), axis=0, keepdims=True
            )

    start = lambda item: item.start()

    def pass_on(kind, distances):
        for r in distances:
            for off in offsets_at(r):
                handle(off, kind, start, True)

    pass_on(0, [0])
    centers = c_ref[...].astype(f32)
    center_len = jnp.sqrt(jnp.sum(centers * centers, axis=1, keepdims=True) + EPSILON)
    len_ref[...] = center_len
    cn_ref[...] = ((centers / center_len).astype(bf16) * LOGIT_SCALE).astype(bf16)
    cnt_ref[...] = jnp.transpose(cn_ref[...])
    for r in range(1, depth):
        pass_on(0, [r])
        pass_on(1, [r - 1])
    score(0, 0)
    pass_on(1, [depth - 1])
    score(1, 0)
    pass_on(2, range(depth))
    score(0, 1)
    score(1, 1)
    pass_on(3, range(depth - 1))
    score(0, 2)
    score(1, 2)
    pass_on(3, [depth - 1])
    score(0, 3)
    score(1, 3)

    started = []

    def share(n, src, target):
        item = copy(held.at[src], landed.at[n], s_sum.at[n], v_sum.at[n], target)
        item.start()
        started.append(item)

    share(0, 0, partners[0])
    started[0].wait_recv()
    held[1] = held[0] + landed[0]
    for n in (1, 2, 3):
        share(n, 1, partners[n])
    for n in (1, 2, 3):
        started[n].wait_recv()
    held[2] = (held[1] + landed[1]) + (landed[2] + landed[3])
    for n in range(4, len(partners)):
        share(n, 2, partners[n])
    for n in range(4, len(partners)):
        started[n].wait_recv()
    total = held[2]
    for n in range(4, len(partners)):
        total = total + landed[n]
    held[3] = total

    def grads(cls, kind):
        j = cls * KINDS + kind
        picks, factors, gains = [], [], []
        for level in range(depth):
            p = j * depth + level
            pick = chosen(rank_ref[p : p + 1, :], most)
            gain = gain_ref[p : p + 1, :]
            factor = gain / held[3, pl.ds(origin(cls, kind, level), 1), :]
            picks.append(pick)
            factors.append(jnp.sum(jnp.where(pick, factor, 0.0), axis=1, keepdims=True))
            gains.append(jnp.sum(jnp.where(pick, gain, 0.0), axis=1, keepdims=True))
        positive = positives(colc_ref[span(j), :], width)
        weights = e_ref[span(j), :] * stacked(factors) - jnp.where(positive, stacked(gains), 0.0)
        weights = weights.astype(bf16)
        w_ref[span(j), :] = weights
        returned = jnp.dot(weights, cn_ref[...], preferred_element_type=f32).astype(bf16)
        for level in range(depth):
            r_ref[j * depth + level] = lax.dot_general(
                one_hot(picks[level]),
                returned[level * most : (level + 1) * most],
                (((0,), (0,)), ((), ())),
                preferred_element_type=f32,
            ).astype(bf16)

    def center_rows(n, pieces):
        size = width // pieces
        at = slice(n * size, (n + 1) * size)
        grad = LOGIT_SCALE * lax.dot_general(
            w_ref[:, at], xc_ref[...], (((0,), (0,)), ((), ())), preferred_element_type=f32
        )
        lens = len_ref[at, :]
        unit = c_ref[at, :].astype(f32) / lens
        along = jnp.sum(unit * grad, axis=1, keepdims=True)
        cg_ref[at, :] = ((grad - unit * along) / lens).astype(bf16)

    def to_sibling(kind, level):
        slot = kind * depth + level
        return copy(
            r_ref.at[(KINDS + kind) * depth + level], rs.at[slot], s_sib.at[slot], v_sib.at[slot], place.sibling()
        )

    def to_second(kind, level):
        slot = (kind & 1) * depth + level
        return copy(tx2.at[slot], rx2.at[slot], s2.at[slot], v2.at[slot], place.second())

    def to_first(level):
        return copy(tx1.at[level], rx1.at[level], s1.at[level], v1.at[level], place.first())

    def to_up(slot):
        return copy(txz.at[slot], rxu.at[slot], sz.at[slot], vu.at[slot], place.up())

    def to_down(slot):
        return copy(txz.at[slot], rxd.at[slot], sz.at[slot], vd.at[slot], place.down())

    def own_sum(kind, level):
        to_sibling(kind, level).wait_recv()
        slot = kind * depth + level
        return r_ref[slot].astype(f32) + rs[slot].astype(f32)

    upper = lax.div(2 * z, depth)
    far_first = [upper * k + (1 - upper) * (depth - 1 - k) for k in range(depth)]

    def give_sibling(kind):
        grads(1, kind)
        for level in far_first:
            to_sibling(kind, level).start()

    for kind in (3, 2):
        give_sibling(kind)
        grads(0, kind)
        for level in far_first:
            tx2[(kind & 1) * depth + level] = own_sum(kind, level).astype(bf16)
            to_second(kind, level).start()
    give_sibling(1)
    grads(0, 1)
    for level in far_first:
        total = own_sum(1, level)
        to_second(3, level).wait_recv()
        tx1[level] = (total + rx2[depth + level].astype(f32)).astype(bf16)
        to_first(level).start()
    give_sibling(0)
    grads(0, 0)
    center_rows(0, 4)

    def gathered_sum(level):
        total = own_sum(0, level)
        to_second(2, level).wait_recv()
        to_first(level).wait_recv()
        return total + rx2[level].astype(f32) + rx1[level].astype(f32)

    for r in range(depth - 1, 0, -1):
        for off in offsets_at(r):

            def cross_z():
                slot = z + off
                item = to_up(slot) if off > 0 else to_down(slot)
                txz[slot] = gathered_sum(slot).astype(bf16)

                @pl.when(z > 0 if off > 0 else z < depth - 1)
                def _():
                    item.wait_recv()
                    arriving = rxu if off > 0 else rxd
                    txz[slot] = (txz[slot].astype(f32) + arriving[slot].astype(f32)).astype(bf16)

                item.start()

            place.when(off, cross_z)
    for n in (1, 2, 3):
        center_rows(n, 4)

    out_ref[...] = gathered_sum(z)

    @pl.when(z > 0)
    def _():
        to_up(z).wait_recv()
        out_ref[...] += rxu[z].astype(f32)

    @pl.when(z < depth - 1)
    def _():
        to_down(z).wait_recv()
        out_ref[...] += rxd[z].astype(f32)

    widened = x_ref[...].astype(f32)
    lengths = jnp.sqrt(jnp.sum(widened * widened, axis=1, keepdims=True) + EPSILON)
    unit = widened / lengths
    grad = out_ref[...]
    along = jnp.sum(unit * grad, axis=1, keepdims=True)
    out_ref[...] = (grad - unit * along) / lengths
    loss_ref[...] = jnp.log(held[3, pl.ds(place.me, 1), :]) - held[3, pl.ds(place.me + devices, 1), :]

    for r in range(depth + 2):
        for off, kind in events(r):
            handle(off, kind, lambda item: item.wait_send(), False)
    for item in started:
        item.wait_send()
    for level in range(depth):
        for kind in range(KINDS):
            to_sibling(kind, level).wait_send()
        for kind in (3, 2):
            to_second(kind, level).wait_send()
        to_first(level).wait_send()
    for r in range(1, depth):
        for off in offsets_at(r):
            place.when(off, lambda: (to_up if off > 0 else to_down)(z + off).wait_send())


def on_device_dense(depth, most, features, loss_scale, blocks, label_col, block_slot, centers):
    devices = depth * 8
    rows, width = features.shape
    capacity = devices * most
    f32, bf16 = jnp.float32, jnp.bfloat16

    def slots(count):
        return pltpu.VMEM((count, rows, width), bf16)

    def sems(*shape):
        return pltpu.SemaphoreType.DMA(shape)

    loss, feature_grad, center_grad = pl.pallas_call(
        functools.partial(fused_kernel, depth, most),
        out_shape=(
            jax.ShapeDtypeStruct((1, rows), f32),
            jax.ShapeDtypeStruct((rows, width), f32),
            jax.ShapeDtypeStruct(centers.shape, bf16),
        ),
        in_specs=[VMEM] * 6,
        out_specs=(VMEM,) * 3,
        scratch_shapes=[
            pltpu.VMEM((devices, rows + TAG_ROWS, width), bf16),
            pltpu.VMEM(centers.shape, bf16),
            pltpu.VMEM(centers.shape[::-1], bf16),
            pltpu.VMEM((centers.shape[0], 1), f32),
            pltpu.VMEM((capacity, width), bf16),
            pltpu.VMEM((capacity, centers.shape[0]), f32),
            pltpu.VMEM((capacity, centers.shape[0]), bf16),
            pltpu.VMEM((devices, rows), f32),
            pltpu.VMEM((devices, rows), f32),
            pltpu.VMEM((capacity, 1), f32),
            pltpu.VMEM((4, 2 * devices, rows), f32),
            pltpu.VMEM((depth + 3, 2 * devices, rows), f32),
            slots(devices),
            slots(devices // 2),
            slots(depth * 2),
            slots(depth * 2),
            slots(depth),
            slots(depth),
            slots(depth),
            slots(depth),
            slots(depth),
            sems(5, devices),
            sems(devices),
            sems(depth + 3),
            sems(depth + 3),
            sems(devices // 2),
            sems(devices // 2),
            sems(depth * 2),
            sems(depth * 2),
            sems(depth),
            sems(depth),
            sems(depth),
            sems(depth),
            sems(depth),
        ],
        compiler_params=pltpu.CompilerParams(
            collective_id=0, has_side_effects=True, vmem_limit_bytes=VMEM_LIMIT
        ),
        name="partial_softmax",
    )(features, loss_scale[None], blocks, label_col[None], block_slot[None], centers)
    return loss.reshape(-1), feature_grad, center_grad


def chosen_plan(mesh, features, loss_scale, blocks, label_col, block_slot, centers):
    dp_count, groups = mesh.shape["dp"], mesh.shape["grp"]
    rows, picks = blocks.shape
    total = block_slot.shape[0]
    quota = (rows * picks + total - 1) // total
    most = quota + max(1, quota // 2)
    dense = (
        most * 4 >= rows
        and most % 16 == 0
        and rows == 128
        and groups == 4
        and dp_count % 2 == 0
        and total == dp_count * groups
        and total <= 256
        and picks == 8
    )
    args = (features, loss_scale, blocks, label_col, block_slot, centers)
    if dense:
        return on_device_dense(dp_count // 2, most, *args)
    return on_device(*args)


def solution(mesh):
    placed = (
        P(("dp", "grp"), None),
        P(("dp", "grp")),
        P(("dp", "grp"), None),
        P(("dp", "grp")),
        P(),
        P(("dp", "grp"), None),
    )
    return jax.shard_map(
        functools.partial(chosen_plan, mesh),
        mesh=mesh,
        in_specs=placed,
        out_specs=(P(("dp", "grp")), P(("dp", "grp"), None), P(("dp", "grp"), None)),
        check_vma=False,
    )
```

```python
import functools

import jax
import jax.numpy as jnp
from jax import lax
from jax.experimental import pallas as pl
from jax.experimental.pallas import tpu as pltpu
from jax.sharding import PartitionSpec as P

BLOCK = 1024


MARGIN = 0.35
LOGIT_SCALE = 64.0
EPSILON = 1e-06


def normalize(block_w):
    widened = block_w.astype(jnp.float32)
    lengths = jnp.sqrt(jnp.sum(widened * widened, axis=1) + EPSILON)
    unit_rows = widened / lengths[:, None]
    return (unit_rows.astype(jnp.bfloat16), unit_rows, lengths)


def normalize_block(block_w):
    squares = jnp.einsum("re,re->r", block_w, block_w, preferred_element_type=jnp.float32)
    lengths = jnp.sqrt(squares + EPSILON)
    unit_rows = block_w.astype(jnp.float32) / lengths[:, None]
    scaled = unit_rows.astype(jnp.bfloat16) * LOGIT_SCALE
    return (scaled, unit_rows, lengths)


def block_logits(rows_x, scaled_centers, columns):
    width = scaled_centers.shape[0]
    scores = lax.dot_general(
        rows_x, scaled_centers, (((1,), (1,)), ((), ())), preferred_element_type=jnp.float32
    )
    row_iota = jnp.arange(rows_x.shape[0], dtype=jnp.int32)
    target_cols = jnp.where(columns >= 0, columns, width)
    scores = scores.at[row_iota, target_cols].add(-LOGIT_SCALE * MARGIN, mode="drop")
    picked = jnp.where(columns >= 0, scores[row_iota, jnp.maximum(columns, 0)], 0.0)
    return (scores, picked)


def center_terms(exps, factor, columns, gains, rows_x, scaled_centers, unit_rows, lengths):
    width = scaled_centers.shape[0]
    row_iota = jnp.arange(exps.shape[0], dtype=jnp.int32)
    target_cols = jnp.where(columns >= 0, columns, width)
    weights = exps * factor[:, None]
    weights = (
        weights.at[row_iota, target_cols]
        .add(-gains.astype(jnp.float32), mode="drop")
        .astype(jnp.bfloat16)
    )
    returned = jnp.dot(weights, scaled_centers, preferred_element_type=jnp.float32)
    scaled_rows = rows_x * LOGIT_SCALE
    unit_grad = lax.dot_general(
        weights, scaled_rows, (((0,), (0,)), ((), ())), preferred_element_type=jnp.float32
    )
    along_unit = jnp.einsum("re,re->r", unit_rows, unit_grad)
    grad_rows = ((unit_grad - unit_rows * along_unit[:, None]) / lengths[:, None]).astype(
        jnp.bfloat16
    )
    return (returned, grad_rows)


def route_rows(rows_out, gains_out, sample_tags, col_tags):
    return (
        lax.all_to_all(
            lax.all_to_all(rows_out, "dp", split_axis=2, concat_axis=2, tiled=True),
            "grp",
            split_axis=1,
            concat_axis=1,
            tiled=True,
        ),
        lax.all_to_all(
            lax.all_to_all(gains_out, "dp", split_axis=2, concat_axis=2, tiled=True),
            "grp",
            split_axis=1,
            concat_axis=1,
            tiled=True,
        ),
        lax.all_to_all(
            lax.all_to_all(sample_tags, "dp", split_axis=2, concat_axis=2, tiled=True),
            "grp",
            split_axis=1,
            concat_axis=1,
            tiled=True,
        ),
        lax.all_to_all(
            lax.all_to_all(col_tags, "dp", split_axis=2, concat_axis=2, tiled=True),
            "grp",
            split_axis=1,
            concat_axis=1,
            tiled=True,
        ),
    )


def route_grads(returned):
    return lax.all_to_all(
        lax.all_to_all(returned, "dp", split_axis=2, concat_axis=2, tiled=True),
        "grp",
        split_axis=1,
        concat_axis=1,
        tiled=True,
    )


def on_device(features, loss_scale, blocks, label_col, block_slot, centers):
    dp_count = lax.axis_size("dp")
    groups = lax.axis_size("grp")
    sample_count, feature_width = features.shape
    pick_count = blocks.shape[1]
    block_total = block_slot.shape[0]
    per_device = centers.shape[0] // BLOCK
    quota = (sample_count * pick_count + block_total - 1) // block_total
    capacity_most = quota + max(1, quota // 2)
    pair_count = sample_count * pick_count
    layout = (per_device, groups, dp_count, capacity_most)
    slot_total = per_device * groups * dp_count * capacity_most
    capacity = groups * dp_count * capacity_most
    normed_feat, unit_feat, feat_norm = normalize(features)
    flat_blocks = blocks.reshape(-1)
    matches = flat_blocks[:, None] == lax.broadcasted_iota(jnp.int32, (pair_count, block_total), 1)
    slot_ids = jnp.sum(jnp.where(matches, block_slot[None, :], 0), axis=1)
    owner_flat = slot_ids // per_device
    local_block = slot_ids % per_device
    owner_grp = owner_flat % groups
    owner_dp = owner_flat // groups
    sample_of = lax.broadcasted_iota(jnp.int32, (sample_count, pick_count), 0).reshape(-1)
    pick_of = lax.broadcasted_iota(jnp.int32, (sample_count, pick_count), 1).reshape(-1)
    earlier = (flat_blocks[:, None] == flat_blocks[None, :]) & (
        sample_of[None, :] < sample_of[:, None]
    )
    rank_of = jnp.sum(earlier.astype(jnp.int32), axis=1)
    places = ((local_block * groups + owner_grp) * dp_count + owner_dp) * capacity_most + rank_of
    rows_out = (
        jnp.zeros((slot_total, feature_width), jnp.bfloat16)
        .at[places]
        .set(jnp.repeat(normed_feat, pick_count, axis=0))
    )
    gains_out = (
        jnp.zeros((slot_total,), jnp.bfloat16).at[places].set(jnp.repeat(loss_scale, pick_count))
    )
    sample_tags = jnp.full((slot_total,), -1, jnp.int32).at[places].set(sample_of)
    col_values = jnp.where(pick_of == 0, jnp.repeat(label_col, pick_count), -1)
    col_tags = jnp.full((slot_total,), -1, jnp.int32).at[places].set(col_values)
    rows_in, gains_in, samples_in, cols_in = route_rows(
        rows_out.reshape(layout + (feature_width,)),
        gains_out.reshape(layout),
        sample_tags.reshape(layout),
        col_tags.reshape(layout),
    )
    local_idx = 0
    scaled_centers, unit_rows, lengths = normalize_block(centers)
    rows_x = rows_in[local_idx].reshape(capacity, feature_width)
    columns = cols_in[local_idx].reshape(capacity)
    scores, picked = block_logits(rows_x, scaled_centers, columns)
    tag_rows = samples_in[local_idx].reshape(capacity)
    gains = gains_in[local_idx].reshape(capacity)
    local_data = [
        (scores, picked, rows_x, scaled_centers, unit_rows, lengths, gains, tag_rows, columns)
    ]
    entry = local_data[0]
    highest = jnp.max(entry[0], axis=1)
    exps = jnp.exp(entry[0] - highest[:, None])
    exps_list = [exps]
    highs = [highest]
    totals = [jnp.sum(exps, axis=1)]
    picks_list = [entry[1]]
    back_high, back_total, back_pick = (
        lax.all_to_all(
            lax.all_to_all(
                jnp.stack(highs).reshape(layout), "dp", split_axis=2, concat_axis=2, tiled=True
            ),
            "grp",
            split_axis=1,
            concat_axis=1,
            tiled=True,
        ),
        lax.all_to_all(
            lax.all_to_all(
                jnp.stack(totals).reshape(layout), "dp", split_axis=2, concat_axis=2, tiled=True
            ),
            "grp",
            split_axis=1,
            concat_axis=1,
            tiled=True,
        ),
        lax.all_to_all(
            lax.all_to_all(
                jnp.stack(picks_list).reshape(layout), "dp", split_axis=2, concat_axis=2, tiled=True
            ),
            "grp",
            split_axis=1,
            concat_axis=1,
            tiled=True,
        ),
    )
    pair_high = back_high.reshape(-1)[places].reshape(sample_count, pick_count)
    pair_total = back_total.reshape(-1)[places].reshape(sample_count, pick_count)
    pair_pick = back_pick.reshape(-1)[places].reshape(sample_count, pick_count)
    sample_peak = jnp.max(pair_high, axis=1)
    sample_denom = jnp.sum(pair_total * jnp.exp(pair_high - sample_peak[:, None]), axis=1)
    target = jnp.sum(pair_pick, axis=1)
    peak_out = (
        jnp.zeros((slot_total,), jnp.float32).at[places].set(jnp.repeat(sample_peak, pick_count))
    )
    denom_out = (
        jnp.ones((slot_total,), jnp.float32).at[places].set(jnp.repeat(sample_denom, pick_count))
    )
    peak_in, denom_in = (
        lax.all_to_all(
            lax.all_to_all(peak_out.reshape(layout), "dp", split_axis=2, concat_axis=2, tiled=True),
            "grp",
            split_axis=1,
            concat_axis=1,
            tiled=True,
        ),
        lax.all_to_all(
            lax.all_to_all(
                denom_out.reshape(layout), "dp", split_axis=2, concat_axis=2, tiled=True
            ),
            "grp",
            split_axis=1,
            concat_axis=1,
            tiled=True,
        ),
    )
    local_idx = 0
    row_peak = peak_in[local_idx].reshape(capacity)
    row_denom = denom_in[local_idx].reshape(capacity)
    gains = local_data[local_idx][6].astype(jnp.float32)
    factors = [gains * jnp.exp(highs[local_idx] - row_peak) / row_denom]
    loss_out = sample_peak + jnp.log(sample_denom) - target
    local_idx = 0
    entry = local_data[local_idx]
    returned, grad_rows = center_terms(
        exps_list[local_idx],
        factors[local_idx],
        entry[8],
        entry[6],
        entry[2],
        entry[3],
        entry[4],
        entry[5],
    )
    returned_list = [returned]
    back_grads = route_grads(jnp.stack(returned_list).reshape(layout + (feature_width,)))
    pair_grads = back_grads.reshape(slot_total, feature_width)[places].reshape(
        sample_count, pick_count, feature_width
    )
    unit_fgrad = jnp.sum(pair_grads, axis=1)
    along = jnp.sum(unit_feat * unit_fgrad, axis=1, keepdims=True)
    feature_grad = (unit_fgrad - unit_feat * along) / feat_norm[:, None]
    return (loss_out, feature_grad, grad_rows)


MESH = pl.DeviceIdType.MESH
VMEM = pl.BlockSpec(memory_space=pltpu.VMEM)
TAG_ROWS = 16
SPLIT = 32
VMEM_LIMIT = 56 * 1024 * 1024


class Place:
    def __init__(self, depth):
        dp, grp = lax.axis_index("dp"), lax.axis_index("grp")
        self.depth = depth
        self.z, y = lax.div(dp, 2), lax.rem(dp, 2)
        x, self.c = lax.div(grp, 2), lax.rem(grp, 2)
        self.a = y + self.c * (x - y)
        self.b = x + self.c * (y - x)
        self.me = dp * 4 + grp

    def device(self, z, a, b, c):
        y, x = a + c * (b - a), b + c * (a - b)
        return (z * 2 + y, x * 2 + c)

    def origin(self, z, a, b, c):
        dp, grp = self.device(z, a, b, c)
        return dp * 4 + grp

    def up(self):
        return self.device(self.z + 1, self.a, self.b, self.c)

    def down(self):
        return self.device(self.z - 1, self.a, self.b, self.c)

    def first(self):
        return self.device(self.z, 1 - self.a, self.b, self.c)

    def second(self):
        return self.device(self.z, self.a, 1 - self.b, self.c)

    def sibling(self):
        return self.device(self.z, self.b, self.a, 1 - self.c)

    def inside(self, offset):
        if offset == 0:
            return None
        return self.z + offset < self.depth if offset > 0 else self.z + offset >= 0

    def when(self, offset, body):
        if offset == 0:
            body()
        else:
            pl.when(self.inside(offset))(body)


def offsets_at(distance):
    return [0] if distance == 0 else [-distance, distance]


UP, DOWN, FIRST, SECOND, SIB = range(5)
KINDS = 4


def chosen(rank, most):
    shape = (most, rank.shape[1])
    return lax.broadcasted_iota(jnp.int32, shape, 0).astype(jnp.float32) == rank


def one_hot(pick):
    return jnp.where(pick, 1.0, 0.0).astype(jnp.bfloat16)


def positives(columns, width):
    shape = (columns.shape[0], width)
    return lax.broadcasted_iota(jnp.int32, shape, 1).astype(jnp.float32) == columns


def fused_kernel(
    depth, most,
    x_ref, scale_ref, blocks_ref, label_ref, slot_ref, c_ref,
    loss_ref, out_ref, cg_ref,
    g_ref, cn_ref, cnt_ref, len_ref, xc_ref, e_ref, w_ref, rank_ref, gain_ref, colc_ref, held, landed,
    r_ref, rs, tx2, rx2, tx1, rx1, txz, rxu, rxd,
    send, recv, s_sum, v_sum, s_sib, v_sib, s2, v2, s1, v1, sz, vu, vd,
):
    f32, bf16 = jnp.float32, jnp.bfloat16
    place = Place(depth)
    z, a, b, c = place.z, place.a, place.b, place.c
    rows, devices = x_ref.shape[0], g_ref.shape[0]
    width = c_ref.shape[0]
    turns = [place.device(lax.rem(z + k, depth), a, b, c) for k in range(1, depth)]
    corner = place.device(z, 1 - a, 1 - b, c)
    partners = [place.sibling(), place.first(), place.second(), corner] + turns
    barrier = pltpu.get_barrier_semaphore()
    for target in partners:
        pl.semaphore_signal(barrier, inc=1, device_id=target, device_id_type=MESH)

    widened = x_ref[...].astype(f32)
    lengths = jnp.sqrt(jnp.sum(widened * widened, axis=1, keepdims=True) + EPSILON)
    g_ref[place.me, 0:rows, :] = (widened / lengths).astype(bf16)
    label = label_ref[...]
    high = lax.div(label, SPLIT)
    tags = jnp.concatenate(
        [
            blocks_ref[...].astype(f32),
            high.astype(f32),
            (label - high * SPLIT).astype(f32),
            scale_ref[...].astype(f32),
            jnp.zeros((TAG_ROWS - 11, rows), f32),
        ],
        axis=0,
    )
    g_ref[place.me, rows : rows + TAG_ROWS, :] = jnp.zeros((TAG_ROWS, x_ref.shape[1]), bf16)
    g_ref[place.me, rows : rows + TAG_ROWS, 0:rows] = tags.astype(bf16)
    slots = slot_ref[...]
    mine = jnp.sum(
        jnp.where(slots == place.me, lax.broadcasted_iota(jnp.int32, slots.shape, 1), 0).astype(f32),
        axis=1,
        keepdims=True,
    )
    pl.semaphore_wait(barrier, len(partners))

    def copy(src, dst, send_sem, recv_sem, target):
        return pltpu.make_async_remote_copy(
            src_ref=src, dst_ref=dst, send_sem=send_sem, recv_sem=recv_sem, device_id=target, device_id_type=MESH
        )

    def package(slot, way, target):
        return copy(g_ref.at[slot], g_ref.at[slot], send.at[way, slot], recv.at[slot], target)

    def arrived(slot):
        package(slot, SIB, place.sibling()).wait_recv()

    def origin(cls, kind, level):
        if cls == 0:
            return place.origin(level, 1 - a if kind & 1 else a, 1 - b if kind & 2 else b, c)
        return place.origin(level, 1 - b if kind & 1 else b, 1 - a if kind & 2 else a, 1 - c)

    def handle(off, kind, act, wait):
        def body():
            slot = origin(0, kind, z + off)
            if wait and (off != 0 or kind != 0):
                arrived(slot)
            if kind == 0 and off <= 0:
                pl.when(z < depth - 1)(lambda: act(package(slot, UP, place.up())))
            if kind == 0 and off >= 0:
                pl.when(z > 0)(lambda: act(package(slot, DOWN, place.down())))
            if kind < 2:
                act(package(slot, SECOND, place.second()))
            if kind < 1:
                act(package(slot, FIRST, place.first()))
            act(package(slot, SIB, place.sibling()))

        place.when(off, body)

    def events(r):
        if r < depth:
            for off in offsets_at(r):
                yield off, 0
        if 1 <= r <= depth:
            for off in offsets_at(r - 1):
                yield off, 1
                yield off, 2
        if 2 <= r <= depth + 1:
            for off in offsets_at(r - 2):
                yield off, 3

    def span(j, level=None):
        if level is None:
            return slice(j * depth * most, (j + 1) * depth * most)
        return slice((j * depth + level) * most, (j * depth + level + 1) * most)

    def stacked(parts):
        return jnp.concatenate(parts, axis=0)

    def score(cls, kind):
        j = cls * KINDS + kind
        levels = range(depth)
        where_from = [origin(cls, kind, level) for level in levels]
        if cls == 1:
            for o in where_from:
                arrived(o)
        tagged = [g_ref[o, rows : rows + TAG_ROWS, 0:rows].astype(f32) for o in where_from]
        hits = [jnp.where(t[0:8] == mine, 1.0, 0.0) for t in tagged]
        wanted = stacked([jnp.sum(hit, axis=0, keepdims=True) for hit in hits])
        shape = (rows, rows)
        earlier = lax.broadcasted_iota(jnp.int32, shape, 0) < lax.broadcasted_iota(jnp.int32, shape, 1)
        padded = stacked([wanted, jnp.zeros((16 - depth % 16, rows), f32)]).astype(bf16)
        ahead = jnp.dot(padded, one_hot(earlier), preferred_element_type=f32)[0:depth]
        rank = jnp.where(wanted > 0.0, ahead, -1.0)
        picks, columns = [], []
        for level in levels:
            p = j * depth + level
            rank_ref[p : p + 1, :] = rank[level : level + 1]
            gain_ref[p : p + 1, :] = tagged[level][10:11]
            pick = chosen(rank[level : level + 1], most)
            column = jnp.where(hits[level][0:1] > 0.0, tagged[level][8:9] * SPLIT + tagged[level][9:10] + 1.0, 0.0)
            picks.append(pick)
            columns.append(jnp.sum(jnp.where(pick, column, 0.0), axis=1, keepdims=True) - 1.0)
            xc_ref[span(j, level), :] = jnp.dot(
                one_hot(pick), g_ref[where_from[level], 0:rows, :], preferred_element_type=f32
            ).astype(bf16)
        columns = stacked(columns)
        colc_ref[span(j), :] = columns
        scores = lax.dot_general(
            xc_ref[span(j), :], cnt_ref[...], (((1,), (0,)), ((), ())), preferred_element_type=f32
        )
        positive = positives(columns, width)
        scores = scores - jnp.where(positive, LOGIT_SCALE * MARGIN, 0.0)
        exps = jnp.exp(scores)
        e_ref[span(j), :] = exps
        sums = jnp.sum(exps, axis=1, keepdims=True)
        target = jnp.sum(jnp.where(positive, scores, 0.0), axis=1, keepdims=True)
        for level in levels:
            at = slice(level * most, (level + 1) * most)
            o = where_from[level]
            held[0, pl.ds(o, 1), :] = jnp.sum(jnp.where(picks[level], sums[at], 0.0), axis=0, keepdims=True)
            held[0, pl.ds(o + devices, 1), :] = jnp.sum(
                jnp.where(picks[level], target[at], 0.0), axis=0, keepdims=True
            )

    start = lambda item: item.start()

    def pass_on(kind, distances):
        for r in distances:
            for off in offsets_at(r):
                handle(off, kind, start, True)

    pass_on(0, [0])
    centers = c_ref[...].astype(f32)
    center_len = jnp.sqrt(jnp.sum(centers * centers, axis=1, keepdims=True) + EPSILON)
    len_ref[...] = center_len
    cn_ref[...] = ((centers / center_len).astype(bf16) * LOGIT_SCALE).astype(bf16)
    cnt_ref[...] = jnp.transpose(cn_ref[...])
    for r in range(1, depth):
        pass_on(0, [r])
        pass_on(1, [r - 1])
    score(0, 0)
    pass_on(1, [depth - 1])
    score(1, 0)
    pass_on(2, range(depth))
    score(0, 1)
    score(1, 1)
    pass_on(3, range(depth - 1))
    score(0, 2)
    score(1, 2)
    pass_on(3, [depth - 1])
    score(0, 3)
    score(1, 3)

    started = []

    def share(n, src, target):
        item = copy(held.at[src], landed.at[n], s_sum.at[n], v_sum.at[n], target)
        item.start()
        started.append(item)

    share(0, 0, partners[0])
    started[0].wait_recv()
    held[1] = held[0] + landed[0]
    for n in (1, 2, 3):
        share(n, 1, partners[n])
    for n in (1, 2, 3):
        started[n].wait_recv()
    held[2] = (held[1] + landed[1]) + (landed[2] + landed[3])
    for n in range(4, len(partners)):
        share(n, 2, partners[n])
    for n in range(4, len(partners)):
        started[n].wait_recv()
    total = held[2]
    for n in range(4, len(partners)):
        total = total + landed[n]
    held[3] = total

    def grads(cls, kind):
        j = cls * KINDS + kind
        picks, factors, gains = [], [], []
        for level in range(depth):
            p = j * depth + level
            pick = chosen(rank_ref[p : p + 1, :], most)
            gain = gain_ref[p : p + 1, :]
            factor = gain / held[3, pl.ds(origin(cls, kind, level), 1), :]
            picks.append(pick)
            factors.append(jnp.sum(jnp.where(pick, factor, 0.0), axis=1, keepdims=True))
            gains.append(jnp.sum(jnp.where(pick, gain, 0.0), axis=1, keepdims=True))
        positive = positives(colc_ref[span(j), :], width)
        weights = e_ref[span(j), :] * stacked(factors) - jnp.where(positive, stacked(gains), 0.0)
        weights = weights.astype(bf16)
        w_ref[span(j), :] = weights
        returned = jnp.dot(weights, cn_ref[...], preferred_element_type=f32).astype(bf16)
        for level in range(depth):
            r_ref[j * depth + level] = lax.dot_general(
                one_hot(picks[level]),
                returned[level * most : (level + 1) * most],
                (((0,), (0,)), ((), ())),
                preferred_element_type=f32,
            ).astype(bf16)

    def center_rows(n, pieces):
        size = width // pieces
        at = slice(n * size, (n + 1) * size)
        grad = LOGIT_SCALE * lax.dot_general(
            w_ref[:, at], xc_ref[...], (((0,), (0,)), ((), ())), preferred_element_type=f32
        )
        lens = len_ref[at, :]
        unit = c_ref[at, :].astype(f32) / lens
        along = jnp.sum(unit * grad, axis=1, keepdims=True)
        cg_ref[at, :] = ((grad - unit * along) / lens).astype(bf16)

    def to_sibling(kind, level):
        slot = kind * depth + level
        return copy(
            r_ref.at[(KINDS + kind) * depth + level], rs.at[slot], s_sib.at[slot], v_sib.at[slot], place.sibling()
        )

    def to_second(kind, level):
        slot = (kind & 1) * depth + level
        return copy(tx2.at[slot], rx2.at[slot], s2.at[slot], v2.at[slot], place.second())

    def to_first(level):
        return copy(tx1.at[level], rx1.at[level], s1.at[level], v1.at[level], place.first())

    def to_up(slot):
        return copy(txz.at[slot], rxu.at[slot], sz.at[slot], vu.at[slot], place.up())

    def to_down(slot):
        return copy(txz.at[slot], rxd.at[slot], sz.at[slot], vd.at[slot], place.down())

    def own_sum(kind, level):
        to_sibling(kind, level).wait_recv()
        slot = kind * depth + level
        return r_ref[slot].astype(f32) + rs[slot].astype(f32)

    upper = lax.div(2 * z, depth)
    far_first = [upper * k + (1 - upper) * (depth - 1 - k) for k in range(depth)]

    def give_sibling(kind):
        grads(1, kind)
        for level in far_first:
            to_sibling(kind, level).start()

    for kind in (3, 2):
        give_sibling(kind)
        grads(0, kind)
        for level in far_first:
            tx2[(kind & 1) * depth + level] = own_sum(kind, level).astype(bf16)
            to_second(kind, level).start()
    give_sibling(1)
    grads(0, 1)
    for level in far_first:
        total = own_sum(1, level)
        to_second(3, level).wait_recv()
        tx1[level] = (total + rx2[depth + level].astype(f32)).astype(bf16)
        to_first(level).start()
    give_sibling(0)
    grads(0, 0)
    center_rows(0, 4)

    def gathered_sum(level):
        total = own_sum(0, level)
        to_second(2, level).wait_recv()
        to_first(level).wait_recv()
        return total + rx2[level].astype(f32) + rx1[level].astype(f32)

    for r in range(depth - 1, 0, -1):
        for off in offsets_at(r):

            def cross_z():
                slot = z + off
                item = to_up(slot) if off > 0 else to_down(slot)
                txz[slot] = gathered_sum(slot).astype(bf16)

                @pl.when(z > 0 if off > 0 else z < depth - 1)
                def _():
                    item.wait_recv()
                    arriving = rxu if off > 0 else rxd
                    txz[slot] = (txz[slot].astype(f32) + arriving[slot].astype(f32)).astype(bf16)

                item.start()

            place.when(off, cross_z)
    for n in (1, 2, 3):
        center_rows(n, 4)

    out_ref[...] = gathered_sum(z)

    @pl.when(z > 0)
    def _():
        to_up(z).wait_recv()
        out_ref[...] += rxu[z].astype(f32)

    @pl.when(z < depth - 1)
    def _():
        to_down(z).wait_recv()
        out_ref[...] += rxd[z].astype(f32)

    loss_ref[...] = jnp.log(held[3, pl.ds(place.me, 1), :]) - held[3, pl.ds(place.me + devices, 1), :]

    for r in range(depth + 2):
        for off, kind in events(r):
            handle(off, kind, lambda item: item.wait_send(), False)
    for item in started:
        item.wait_send()
    for level in range(depth):
        for kind in range(KINDS):
            to_sibling(kind, level).wait_send()
        for kind in (3, 2):
            to_second(kind, level).wait_send()
        to_first(level).wait_send()
    for r in range(1, depth):
        for off in offsets_at(r):
            place.when(off, lambda: (to_up if off > 0 else to_down)(z + off).wait_send())


def finish_kernel(loss_ref, grad_ref, cg_ref, x_ref, loss_out, out_ref, cg_out):
    loss_out[...] = loss_ref[...]
    cg_out[...] = cg_ref[...]
    widened = x_ref[...].astype(jnp.float32)
    lengths = jnp.sqrt(jnp.sum(widened * widened, axis=1, keepdims=True) + EPSILON)
    unit = widened / lengths
    grad = grad_ref[...]
    along = jnp.sum(unit * grad, axis=1, keepdims=True)
    out_ref[...] = (grad - unit * along) / lengths


def finish(loss, unit_grad, center_grad, features):
    loss, feature_grad, center_grad = pl.pallas_call(
        finish_kernel,
        out_shape=tuple(jax.ShapeDtypeStruct(part.shape, part.dtype) for part in (loss, unit_grad, center_grad)),
        in_specs=[VMEM] * 4,
        out_specs=(VMEM,) * 3,
        name="finish",
    )(loss, unit_grad, center_grad, features)
    return loss.reshape(-1), feature_grad, center_grad


def on_device_dense(depth, most, features, loss_scale, blocks, label_col, block_slot, centers):
    devices = depth * 8
    rows, width = features.shape
    capacity = devices * most
    f32, bf16 = jnp.float32, jnp.bfloat16

    def slots(count):
        return pltpu.VMEM((count, rows, width), bf16)

    def sems(*shape):
        return pltpu.SemaphoreType.DMA(shape)

    loss, unit_grad, center_grad = pl.pallas_call(
        functools.partial(fused_kernel, depth, most),
        out_shape=(
            jax.ShapeDtypeStruct((1, rows), f32),
            jax.ShapeDtypeStruct((rows, width), f32),
            jax.ShapeDtypeStruct(centers.shape, bf16),
        ),
        in_specs=[VMEM] * 6,
        out_specs=(VMEM,) * 3,
        scratch_shapes=[
            pltpu.VMEM((devices, rows + TAG_ROWS, width), bf16),
            pltpu.VMEM(centers.shape, bf16),
            pltpu.VMEM(centers.shape[::-1], bf16),
            pltpu.VMEM((centers.shape[0], 1), f32),
            pltpu.VMEM((capacity, width), bf16),
            pltpu.VMEM((capacity, centers.shape[0]), f32),
            pltpu.VMEM((capacity, centers.shape[0]), bf16),
            pltpu.VMEM((devices, rows), f32),
            pltpu.VMEM((devices, rows), f32),
            pltpu.VMEM((capacity, 1), f32),
            pltpu.VMEM((4, 2 * devices, rows), f32),
            pltpu.VMEM((depth + 3, 2 * devices, rows), f32),
            slots(devices),
            slots(devices // 2),
            slots(depth * 2),
            slots(depth * 2),
            slots(depth),
            slots(depth),
            slots(depth),
            slots(depth),
            slots(depth),
            sems(5, devices),
            sems(devices),
            sems(depth + 3),
            sems(depth + 3),
            sems(devices // 2),
            sems(devices // 2),
            sems(depth * 2),
            sems(depth * 2),
            sems(depth),
            sems(depth),
            sems(depth),
            sems(depth),
            sems(depth),
        ],
        compiler_params=pltpu.CompilerParams(
            collective_id=0, has_side_effects=True, vmem_limit_bytes=VMEM_LIMIT
        ),
        name="partial_softmax",
    )(features, loss_scale[None], blocks.T, label_col[None], block_slot[None], centers)
    return finish(loss, unit_grad, center_grad, features)


def chosen_plan(mesh, features, loss_scale, blocks, label_col, block_slot, centers):
    dp_count, groups = mesh.shape["dp"], mesh.shape["grp"]
    rows, picks = blocks.shape
    total = block_slot.shape[0]
    quota = (rows * picks + total - 1) // total
    most = quota + max(1, quota // 2)
    dense = (
        most * 4 >= rows
        and most % 16 == 0
        and rows == 128
        and groups == 4
        and dp_count % 2 == 0
        and total == dp_count * groups
        and total <= 256
        and picks == 8
    )
    args = (features, loss_scale, blocks, label_col, block_slot, centers)
    if dense:
        return on_device_dense(dp_count // 2, most, *args)
    return on_device(*args)


def solution(mesh):
    placed = (
        P(("dp", "grp"), None),
        P(("dp", "grp")),
        P(("dp", "grp"), None),
        P(("dp", "grp")),
        P(),
        P(("dp", "grp"), None),
    )
    return jax.shard_map(
        functools.partial(chosen_plan, mesh),
        mesh=mesh,
        in_specs=placed,
        out_specs=(P(("dp", "grp")), P(("dp", "grp"), None), P(("dp", "grp"), None)),
        check_vma=False,
    )
```
